32 devices in a mesh: groups: 2 (over y), rows: 4 (over z), feat: 2 (over x), sub: 2 (over core).
Axes of the slice: x: 2, y: 2, z: 4, core: 2. Of those that a mesh axis runs over, the one named last changes fastest.
Arguments:
- embeddings: float32 [8192, 768], P(('groups', 'rows', 'feat', 'sub')), parts along dimension 0, may hold values from -64 to 64
- assign: int32 [8192], P(('groups', 'rows', 'feat', 'sub')), parts along dimension 0, may hold values from 0 to 1023, as said below
- order: int32 [8192], P(('groups', 'rows', 'feat', 'sub')), parts along dimension 0, may hold values from 0 to 4095, each once
Outputs:
- dup_score: float32 [8192], P(('groups', 'rows', 'feat', 'sub')), parts along dimension 0
- cent_score: float32 [8192], P(('groups', 'rows', 'feat', 'sub')), parts along dimension 0
- centroids: float32 [2048, 768], P(('groups', 'rows', 'feat')), parts along dimension 0
The draws below stay inside these ranges and needn't reach their ends.
There are 2 independent parts, one for each index of `groups`. The reference program is written for one: setup_inputs(seed, part) draws one part's arguments, and reference() takes and returns one part's arrays. A program takes and returns all parts, laid end to end along the dimension named above; each array names one. Nothing has to cross between parts.
Inputs may be any that keep to these rules, and one draw needn't show every extreme that they name: `assign`: cluster k belongs to owner k // 128. Among the 256 rows of one device (aligned blocks), at most 64 rows belong to one owner's clusters; in every block some owner has exactly 64, and one owner has exactly 64 in every block.
All inputs are finite; a program needn't handle non-finite values.
Results may differ from the reference program's by a relative error of at most 0.00061.
Values may be sent and summed in bfloat16 or wider, within the bound.
No kernel may reach another device: no remote copies, remote signals or barrier semaphores. Data moves between devices by JAX's collectives and lax.ppermute only.
A program may use at most 64 MiB of HBM per device.

```python
import math
import jax
import jax.numpy as jnp
from jax import lax

DIM = 768
K = 1024
P_DEV = 256
N_OWN = 8
K_OWN = 128
BUCKET = 1024
NR = 4096


def draw_embeddings(key, part):
    key = jax.random.fold_in(key, 3)
    first, second, third = jax.random.split(key, 3)
    col_scale = jnp.exp(jax.random.uniform(third, (1, DIM), jnp.float32, math.log(0.3), math.log(3.0)))
    base = jnp.clip(jax.random.normal(first, (NR, DIM), jnp.float32), -4.0, 4.0)
    row_scale = jnp.exp(jax.random.uniform(second, (NR, 1), jnp.float32, 0.0, math.log(10.0)))
    return jnp.clip(base * row_scale * col_scale, -64.0, 64.0).astype(jnp.float32)


def draw_assign(key, part):
    key = jax.random.fold_in(key, 7)
    blocks = NR // P_DEV
    capacity = 2 * P_DEV // N_OWN
    keys = jax.random.split(key, blocks + 1)
    fixed = jax.random.randint(keys[0], (), 0, N_OWN).astype(jnp.int32)
    ranking = jnp.arange(N_OWN, dtype=jnp.int32)
    counts = jnp.where(ranking < N_OWN // 4, capacity, jnp.where(ranking < 3 * N_OWN // 4, capacity // 2, 0)).astype(jnp.int32)

    def one_block(block_key):
        key_a, key_b, key_c = jax.random.split(block_key, 3)
        others = jnp.arange(N_OWN - 1, dtype=jnp.int32)
        others = others + (others >= fixed).astype(jnp.int32)
        others = jax.random.permutation(key_a, others)
        listing = jnp.concatenate([fixed[None], others])
        owners_seq = jnp.repeat(listing, counts, total_repeat_length=P_DEV)
        owners_seq = jax.random.permutation(key_b, owners_seq)
        inner = jax.random.randint(key_c, (P_DEV,), 0, K_OWN).astype(jnp.int32)
        return owners_seq * K_OWN + inner
    return jax.vmap(one_block)(keys[1:]).reshape(-1).astype(jnp.int32)


def setup_inputs(seed: int = 0, part: int = 0) -> dict:
    seeds = jax.random.split(jax.random.key(seed), 4)
    own_keys = jax.random.split(jax.random.fold_in(seeds[3], part), 4)
    embeddings = draw_embeddings(jax.random.fold_in(jax.random.fold_in(seeds[3], part), 71), part)
    assign = draw_assign(jax.random.fold_in(jax.random.fold_in(seeds[3], part), 71), part)
    order = jax.random.permutation(own_keys[2], NR).astype(jnp.int32)
    return {"embeddings": embeddings, "assign": assign, "order": order}


EPSILON = 1e-06

def reference(embeddings, assign, order):
    unit = embeddings * lax.rsqrt(lax.optimization_barrier(jnp.sum(embeddings * embeddings, axis=1, keepdims=True)) + EPSILON)
    sums = jax.ops.segment_sum(unit, assign, num_segments=K)
    centroids = sums * lax.rsqrt(lax.optimization_barrier(jnp.sum(sums * sums, axis=1, keepdims=True)) + EPSILON)
    unit_half = unit.astype(jnp.bfloat16)
    cent_score = lax.optimization_barrier(jnp.sum(unit_half.astype(jnp.float32) * centroids[assign], axis=1))
    target = (assign // K_OWN).astype(jnp.int32)
    hits = (target[:, None] == jnp.arange(N_OWN, dtype=jnp.int32)[None, :]).astype(jnp.int32)
    position = lax.optimization_barrier(jnp.sum((jnp.cumsum(hits, axis=0) - hits) * hits, axis=1)).astype(jnp.int32)
    spot = (target * BUCKET + position).astype(jnp.int32)
    table = jnp.full((N_OWN * BUCKET,), -1, jnp.int32).at[spot].set(jnp.arange(NR, dtype=jnp.int32))

    def owner_best(index):
        live = index >= 0
        safe = jnp.maximum(index, 0).astype(jnp.int32)
        vectors = unit_half[safe]
        members = jnp.where(live, assign[safe], -1)
        ranks = order[safe]
        scores = jnp.dot(vectors, vectors.T, preferred_element_type=jnp.float32)
        allowed = (members[:, None] == members[None, :]) & (ranks[None, :] < ranks[:, None]) & live[None, :]
        return lax.optimization_barrier(jnp.max(jnp.where(allowed, scores, -1.0), axis=1))
    best = lax.map(owner_best, table.reshape(N_OWN, BUCKET)).reshape(-1)
    dup_score = best[spot]
    return (dup_score, cent_score, centroids)
```

```python
import functools

import jax
import jax.numpy as jnp
from jax import lax
from jax.experimental import pallas as pl
from jax.experimental.pallas import tpu as pltpu
from jax.sharding import PartitionSpec as P

K = 1024


EPSILON = 1e-06
LANES = 128
META = 16
FULL = 32768.0
STEPS = (32, 16, 8, 4, 2, 1)


def swapped(shard, axis, distance):
    return lax.ppermute(shard, axis, [(i, i ^ 1 << distance) for i in range(lax.axis_size(axis))])


def unit_rows(values):
    return values * lax.rsqrt(jnp.sum(values * values, axis=1, keepdims=True) + EPSILON)


def best_against(q_vec, q_clu, q_ord, k_vec, k_clu, k_ord):
    scores = lax.dot_general(
        q_vec, k_vec, (((1,), (1,)), ((), ())), preferred_element_type=jnp.float32
    )
    allowed = (q_clu[:, None] == k_clu[None, :]) & (k_ord[None, :] < q_ord[:, None])
    return jnp.max(jnp.where(allowed, scores, -1.0), axis=1)


def cluster_sums(vectors, clusters, first_cluster, per_owner):
    local = clusters - first_cluster
    member = (jnp.arange(per_owner, dtype=jnp.int32)[:, None] == local[None, :]).astype(jnp.float32)
    return jnp.dot(
        member, vectors, precision=lax.Precision.HIGHEST, preferred_element_type=jnp.float32
    )


def exchange_all(embeddings, assign, order):
    owners = lax.axis_size("rows") * lax.axis_size("feat")
    rows_dev = embeddings.shape[0]
    width = embeddings.shape[1]
    capacity = 2 * rows_dev // owners
    per_owner = K // owners
    slots = owners * capacity
    here = lax.axis_index(("rows", "feat"))
    unit = unit_rows(embeddings)
    target = assign // per_owner
    hits = (target[:, None] == jnp.arange(owners, dtype=jnp.int32)[None, :]).astype(jnp.int32)
    before = jnp.cumsum(hits, axis=0) - hits
    slot = target * capacity + jnp.sum(before * hits, axis=1)
    send_clu = jnp.full((slots,), -1, jnp.int32).at[slot].set(assign)
    send_ord = jnp.zeros((slots,), jnp.int32).at[slot].set(order)
    send_wide = jnp.zeros((slots, width), jnp.float32).at[slot].set(unit)
    spread = functools.partial(
        lax.all_to_all, axis_name=("rows", "feat"), split_axis=0, concat_axis=0, tiled=True
    )
    wide_vec = spread(send_wide.reshape(owners, capacity, width)).reshape(slots, width)
    got_clu = spread(send_clu.reshape(owners, capacity)).reshape(slots)
    got_ord = spread(send_ord.reshape(owners, capacity)).reshape(slots)
    other_wide, other_clu, other_ord = swapped((wide_vec, got_clu, got_ord), "sub", 0)
    first_cluster = here * per_owner
    own_sums = cluster_sums(wide_vec, got_clu, first_cluster, per_owner)
    pair_sums = cluster_sums(other_wide, other_clu, first_cluster, per_owner)
    own_cent = unit_rows(own_sums + pair_sums)
    got_vec = wide_vec.astype(jnp.bfloat16)
    other_vec = other_wide.astype(jnp.bfloat16)
    block = min(512, slots)
    nblock = slots // block

    def per_block(pieces):
        q_vec, q_clu, q_ord = pieces
        first = best_against(q_vec, q_clu, q_ord, got_vec, got_clu, got_ord)
        second = best_against(q_vec, q_clu, q_ord, other_vec, other_clu, other_ord)
        return jnp.maximum(first, second)

    best = lax.map(
        per_block,
        (
            got_vec.reshape(nblock, block, width),
            got_clu.reshape(nblock, block),
            got_ord.reshape(nblock, block),
        ),
    ).reshape(slots)
    local = jnp.clip(got_clu - here * per_owner, 0, per_owner - 1)
    fits = jnp.dot(
        got_vec.astype(jnp.float32),
        own_cent.T,
        precision=lax.Precision.HIGHEST,
        preferred_element_type=jnp.float32,
    )
    pick = local[:, None] == jnp.arange(per_owner, dtype=jnp.int32)[None, :]
    near = jnp.sum(jnp.where(pick, fits, 0.0), axis=1)
    back_best = spread(best.reshape(owners, capacity))
    back_near = spread(near.reshape(owners, capacity))
    return (back_best.reshape(slots)[slot], back_near.reshape(slots)[slot], own_cent)


def iota(shape, dim):
    return lax.broadcasted_iota(jnp.int32, shape, dim)


def dot_t(a, b):
    return lax.dot_general(a, b, (((1,), (1,)), ((), ())), preferred_element_type=jnp.float32)


def halves(x):
    high = x.astype(jnp.bfloat16)
    return high, (x - high.astype(jnp.float32)).astype(jnp.bfloat16)


def pack_kernel(owners, capacity, per_owner, emb_ref, asg_ref, ord_ref, *outs):
    packs, pos_ref = outs[:owners], outs[owners]
    rows, width = emb_ref.shape
    slots = owners * capacity
    me = lax.axis_index(("rows", "feat"))
    x = emb_ref[...]
    unit = x * lax.rsqrt(jnp.sum(x * x, axis=1, keepdims=True) + EPSILON)
    top = jnp.max(jnp.abs(unit), axis=1, keepdims=True)
    scale = jnp.ones_like(top)
    power = jnp.zeros_like(top)
    for step in STEPS:
        small = top * (scale * 2.0**step) < 1.0
        scale = jnp.where(small, scale * 2.0**step, scale)
        power = jnp.where(small, power + step, power)
    coded = jnp.clip(jnp.round(unit * (scale * FULL)), -FULL, FULL - 1.0)
    high, low = halves(coded)

    asg = asg_ref[...]
    rank = ord_ref[...]
    target = lax.div(asg, jnp.int32(per_owner))
    seat = target ^ me
    hits = iota((owners, rows), 0) == target
    earlier = (iota((rows, rows), 0) < iota((rows, rows), 1)).astype(jnp.bfloat16)
    before = jnp.dot(
        hits.astype(jnp.bfloat16), earlier, preferred_element_type=jnp.float32
    )
    pos = jnp.sum(jnp.where(hits, before, 0.0), axis=0, keepdims=True).astype(jnp.int32)
    pos_ref[...] = pos
    place = (iota((slots, rows), 0) == seat * capacity + pos).astype(jnp.bfloat16)

    power_row = jnp.transpose(jnp.broadcast_to(power, (rows, LANES)))[:1, :]
    facts = jnp.concatenate(
        [
            (asg - target * per_owner + 1).astype(jnp.float32),
            (rank & 255).astype(jnp.float32),
            (rank >> 8).astype(jnp.float32),
            power_row,
            jnp.zeros((4, rows), jnp.float32),
        ],
        axis=0,
    ).astype(jnp.bfloat16)
    facts = dot_t(facts, place)
    for v in range(owners):
        mine = place[v * capacity : (v + 1) * capacity, :]
        block = jnp.dot(mine, high, preferred_element_type=jnp.float32) + jnp.dot(
            mine, low, preferred_element_type=jnp.float32
        )
        block = block.astype(jnp.int32).astype(jnp.int16)
        for c in range(width // LANES):
            packs[v][c * capacity : (c + 1) * capacity, :] = block[:, c * LANES : (c + 1) * LANES]
        notes = facts[:, v * capacity : (v + 1) * capacity]
        notes = jnp.concatenate([notes, jnp.zeros((8, LANES - capacity), jnp.float32)], axis=1)
        notes = jnp.concatenate([notes, jnp.zeros((META - 8, LANES), jnp.float32)], axis=0)
        packs[v][width // LANES * capacity :, :] = notes.astype(jnp.int32).astype(jnp.int16)


def score_kernel(owners, capacity, per_owner, width, *refs):
    count = 2 * owners
    chunks = refs[:count]
    cent_ref, back_ref, high_ref, low_ref = refs[count:]
    tiles = width // LANES
    slots = owners * capacity
    me = lax.axis_index(("rows", "feat"))
    eye = (iota((LANES, LANES), 0) == iota((LANES, LANES), 1)).astype(jnp.float32)
    clu_rows, code_rows, code_cols = [], [], []
    for pair in range(owners):
        notes = [
            ref[tiles * capacity :, :].astype(jnp.int32).astype(jnp.float32)[:8, :capacity]
            for ref in chunks[2 * pair : 2 * pair + 2]
        ]
        notes = jnp.concatenate(notes, axis=1)
        clu = notes[0:1, :] - 1.0
        rank = notes[1:2, :] + 256.0 * notes[2:3, :]
        power = notes[3:4, :]
        scale = jnp.full_like(power, 1.0 / FULL)
        for step in STEPS:
            there = power >= step
            scale = jnp.where(there, scale * 2.0**-step, scale)
            power = jnp.where(there, power - step, power)
        code = jnp.where(clu >= 0.0, clu * 65536.0 + rank, -1.0)
        both = jnp.concatenate([code, scale, jnp.zeros((6, LANES), jnp.float32)], axis=0)
        cols = lax.dot_general(
            eye,
            both,
            (((1,), (1,)), ((), ())),
            precision=lax.Precision.HIGHEST,
            preferred_element_type=jnp.float32,
        )
        clu_rows.append(clu)
        code_rows.append(code)
        code_cols.append(cols[:, 0:1])
        for half in range(2):
            ref = chunks[2 * pair + half]
            first = (2 * pair + half) * capacity
            factor = cols[half * capacity : (half + 1) * capacity, 1:2]
            for c in range(tiles):
                part = ref[c * capacity : (c + 1) * capacity, :]
                high, low = halves(part.astype(jnp.int32).astype(jnp.float32) * factor)
                high_ref[first : first + capacity, c * LANES : (c + 1) * LANES] = high
                low_ref[first : first + capacity, c * LANES : (c + 1) * LANES] = low
    clu_all = jnp.concatenate(clu_rows, axis=1)
    member = (iota((per_owner, 2 * slots), 0).astype(jnp.float32) == clu_all).astype(jnp.bfloat16)
    sums = jnp.dot(member, high_ref[...], preferred_element_type=jnp.float32) + jnp.dot(
        member, low_ref[...], preferred_element_type=jnp.float32
    )
    cent = sums * lax.rsqrt(jnp.sum(sums * sums, axis=1, keepdims=True) + EPSILON)
    cent_ref[...] = cent
    cent_high, cent_low = halves(cent)
    asked = high_ref[:slots, :]
    fits = dot_t(cent_high, asked) + dot_t(cent_low, asked)
    near = jnp.sum(jnp.where(member[:, :slots] > 0, fits, 0.0), axis=0, keepdims=True)
    own_code = jnp.concatenate(code_rows[: owners // 2], axis=1)
    own_base = jnp.concatenate(clu_rows[: owners // 2], axis=1) * 65536.0
    best = jnp.full((1, slots), -1.0, jnp.float32)
    for pair in range(owners):
        scores = dot_t(high_ref[pair * LANES : (pair + 1) * LANES, :], asked)
        code = code_cols[pair]
        allowed = (code >= own_base) & (code < own_code)
        best = jnp.maximum(
            best, jnp.max(jnp.where(allowed, scores, -1.0), axis=0, keepdims=True)
        )
    for v in range(owners):
        part = slice(v * capacity, (v + 1) * capacity)
        back_ref[pl.ds(me ^ v, 1), :] = jnp.concatenate([best[:, part], near[:, part]], axis=1)


def pick_kernel(owners, capacity, per_owner, back_ref, asg_ref, pos_ref, best_ref, near_ref):
    rows = asg_ref.shape[1]
    target = lax.div(asg_ref[...], jnp.int32(per_owner))
    pos = pos_ref[...]
    hits = iota((owners, rows), 0) == target
    back = back_ref[...]
    for first, ref in ((0, best_ref), (capacity, near_ref)):
        place = (iota((LANES, rows), 0) == pos + first).astype(jnp.float32)
        found = jnp.dot(
            back, place, precision=lax.Precision.HIGHEST, preferred_element_type=jnp.float32
        )
        ref[...] = jnp.sum(jnp.where(hits, found, 0.0), axis=0, keepdims=True)


def exchange_pairs(embeddings, assign, order):
    owners = lax.axis_size("rows") * lax.axis_size("feat")
    rows, width = embeddings.shape
    capacity = 2 * rows // owners
    per_owner = K // owners
    slots = owners * capacity
    tall = width // LANES * capacity + META
    assign = assign.reshape(1, rows)
    order = order.reshape(1, rows)
    vmem = pl.BlockSpec(memory_space=pltpu.VMEM)
    *packs, pos = pl.pallas_call(
        functools.partial(pack_kernel, owners, capacity, per_owner),
        out_shape=[jax.ShapeDtypeStruct((tall, LANES), jnp.int16)] * owners
        + [jax.ShapeDtypeStruct((1, rows), jnp.int32)],
        in_specs=[vmem] * 3,
        out_specs=[vmem] * (owners + 1),
        compiler_params=pltpu.CompilerParams(vmem_limit_bytes=32 << 20),
        name="pack",
    )(embeddings, assign, order)
    got = [packs[0]] + [
        lax.ppermute(packs[v], ("rows", "feat"), [(i, i ^ v) for i in range(owners)])
        for v in range(1, owners)
    ]
    other = [swapped(chunk, "sub", 0) for chunk in got]
    cent, back = pl.pallas_call(
        functools.partial(score_kernel, owners, capacity, per_owner, width),
        out_shape=[
            jax.ShapeDtypeStruct((per_owner, width), jnp.float32),
            jax.ShapeDtypeStruct((owners, LANES), jnp.float32),
        ],
        in_specs=[vmem] * (2 * owners),
        out_specs=[vmem] * 2,
        scratch_shapes=[pltpu.VMEM((2 * slots, width), jnp.bfloat16)] * 2,
        compiler_params=pltpu.CompilerParams(vmem_limit_bytes=32 << 20),
        name="score",
    )(*got, *other)
    back = lax.all_to_all(back, ("rows", "feat"), split_axis=0, concat_axis=0, tiled=True)
    best, near = pl.pallas_call(
        functools.partial(pick_kernel, owners, capacity, per_owner),
        out_shape=[jax.ShapeDtypeStruct((1, rows), jnp.float32)] * 2,
        in_specs=[vmem] * 3,
        out_specs=[vmem] * 2,
        name="pick",
    )(back, assign, pos)
    return best.reshape(rows), near.reshape(rows), cent


def body(embeddings, assign, order):
    owners = lax.axis_size("rows") * lax.axis_size("feat")
    rows, width = embeddings.shape
    few = owners == 8 and 2 * rows // owners * 2 == LANES and width % LANES == 0
    return (exchange_pairs if few else exchange_all)(embeddings, assign, order)


def solution(mesh):
    return jax.shard_map(
        body,
        mesh=mesh,
        in_specs=(
            P(("groups", "rows", "feat", "sub"), None),
            P(("groups", "rows", "feat", "sub")),
            P(("groups", "rows", "feat", "sub")),
        ),
        out_specs=(
            P(("groups", "rows", "feat", "sub")),
            P(("groups", "rows", "feat", "sub")),
            P(("groups", "rows", "feat"), None),
        ),
        check_vma=False,
    )
```

```python
import functools

import jax
import jax.numpy as jnp
from jax import lax
from jax.experimental import pallas as pl
from jax.experimental.pallas import tpu as pltpu
from jax.sharding import PartitionSpec as P

K = 1024


EPSILON = 1e-06
LANES = 128
META = 16
FULL = 32768.0
STEPS = (32, 16, 8, 4, 2, 1)
CODE = 65536.0
NONE = -1e30
FIRST = (4, 1, 5, 2, 6, 3, 7, 0)


def swapped(shard, axis, distance):
    return lax.ppermute(shard, axis, [(i, i ^ 1 << distance) for i in range(lax.axis_size(axis))])


def unit_rows(values):
    return values * lax.rsqrt(jnp.sum(values * values, axis=1, keepdims=True) + EPSILON)


def best_against(q_vec, q_clu, q_ord, k_vec, k_clu, k_ord):
    scores = lax.dot_general(
        q_vec, k_vec, (((1,), (1,)), ((), ())), preferred_element_type=jnp.float32
    )
    allowed = (q_clu[:, None] == k_clu[None, :]) & (k_ord[None, :] < q_ord[:, None])
    return jnp.max(jnp.where(allowed, scores, -1.0), axis=1)


def cluster_sums(vectors, clusters, first_cluster, per_owner):
    local = clusters - first_cluster
    member = (jnp.arange(per_owner, dtype=jnp.int32)[:, None] == local[None, :]).astype(jnp.float32)
    return jnp.dot(
        member, vectors, precision=lax.Precision.HIGHEST, preferred_element_type=jnp.float32
    )


def exchange_all(embeddings, assign, order):
    owners = lax.axis_size("rows") * lax.axis_size("feat")
    rows_dev = embeddings.shape[0]
    width = embeddings.shape[1]
    capacity = 2 * rows_dev // owners
    per_owner = K // owners
    slots = owners * capacity
    here = lax.axis_index(("rows", "feat"))
    unit = unit_rows(embeddings)
    target = assign // per_owner
    hits = (target[:, None] == jnp.arange(owners, dtype=jnp.int32)[None, :]).astype(jnp.int32)
    before = jnp.cumsum(hits, axis=0) - hits
    slot = target * capacity + jnp.sum(before * hits, axis=1)
    send_clu = jnp.full((slots,), -1, jnp.int32).at[slot].set(assign)
    send_ord = jnp.zeros((slots,), jnp.int32).at[slot].set(order)
    send_wide = jnp.zeros((slots, width), jnp.float32).at[slot].set(unit)
    spread = functools.partial(
        lax.all_to_all, axis_name=("rows", "feat"), split_axis=0, concat_axis=0, tiled=True
    )
    wide_vec = spread(send_wide.reshape(owners, capacity, width)).reshape(slots, width)
    got_clu = spread(send_clu.reshape(owners, capacity)).reshape(slots)
    got_ord = spread(send_ord.reshape(owners, capacity)).reshape(slots)
    other_wide, other_clu, other_ord = swapped((wide_vec, got_clu, got_ord), "sub", 0)
    first_cluster = here * per_owner
    own_sums = cluster_sums(wide_vec, got_clu, first_cluster, per_owner)
    pair_sums = cluster_sums(other_wide, other_clu, first_cluster, per_owner)
    own_cent = unit_rows(own_sums + pair_sums)
    got_vec = wide_vec.astype(jnp.bfloat16)
    other_vec = other_wide.astype(jnp.bfloat16)
    block = min(512, slots)
    nblock = slots // block

    def per_block(pieces):
        q_vec, q_clu, q_ord = pieces
        first = best_against(q_vec, q_clu, q_ord, got_vec, got_clu, got_ord)
        second = best_against(q_vec, q_clu, q_ord, other_vec, other_clu, other_ord)
        return jnp.maximum(first, second)

    best = lax.map(
        per_block,
        (
            got_vec.reshape(nblock, block, width),
            got_clu.reshape(nblock, block),
            got_ord.reshape(nblock, block),
        ),
    ).reshape(slots)
    local = jnp.clip(got_clu - here * per_owner, 0, per_owner - 1)
    fits = jnp.dot(
        got_vec.astype(jnp.float32),
        own_cent.T,
        precision=lax.Precision.HIGHEST,
        preferred_element_type=jnp.float32,
    )
    pick = local[:, None] == jnp.arange(per_owner, dtype=jnp.int32)[None, :]
    near = jnp.sum(jnp.where(pick, fits, 0.0), axis=1)
    back_best = spread(best.reshape(owners, capacity))
    back_near = spread(near.reshape(owners, capacity))
    return (back_best.reshape(slots)[slot], back_near.reshape(slots)[slot], own_cent)


def iota(shape, dim):
    return lax.broadcasted_iota(jnp.int32, shape, dim)


def dot(a, b):
    return jnp.dot(a, b, preferred_element_type=jnp.float32)


def dot_t(a, b):
    return lax.dot_general(a, b, (((1,), (1,)), ((), ())), preferred_element_type=jnp.float32)


def halves(x):
    high = x.astype(jnp.bfloat16)
    return high, (x - high.astype(jnp.float32)).astype(jnp.bfloat16)


def pack_kernel(owners, capacity, per_owner, emb_ref, asg_ref, ord_ref, *refs):
    packs, slot_hbm = refs[:owners], refs[owners]
    slot_ref, slot_sem = refs[owners + 1 :]
    rows, width = emb_ref.shape
    slots = owners * capacity
    tiles = width // LANES
    me = lax.axis_index(("rows", "feat"))
    asg = asg_ref[...]
    rank = ord_ref[...]
    target = lax.div(asg, jnp.int32(per_owner))
    hits = iota((owners, rows), 0) == target
    earlier = (iota((rows, rows), 0) < iota((rows, rows), 1)).astype(jnp.bfloat16)
    before = dot(hits.astype(jnp.bfloat16), earlier)
    pos = jnp.sum(jnp.where(hits, before, 0.0), axis=0, keepdims=True).astype(jnp.int32)
    slot = (target ^ me) * capacity + pos
    slot_ref[...] = slot
    slot_copy = pltpu.make_async_copy(slot_ref, slot_hbm, slot_sem)
    slot_copy.start()
    place = (iota((slots, rows), 0) == slot).astype(jnp.bfloat16)

    x = emb_ref[...]
    unit = x * lax.rsqrt(jnp.sum(x * x, axis=1, keepdims=True) + EPSILON)
    top = jnp.max(jnp.abs(unit), axis=1, keepdims=True)
    scale = jnp.ones_like(top)
    power = jnp.zeros_like(top)
    for step in STEPS:
        small = top * (scale * 2.0**step) < 1.0
        scale = jnp.where(small, scale * 2.0**step, scale)
        power = jnp.where(small, power + step, power)
    coded = jnp.minimum(jnp.round(unit * (scale * FULL)), FULL - 1.0)
    high, low = halves(coded)
    power_row = jnp.transpose(jnp.broadcast_to(power, (rows, LANES)))[:1, :]
    facts = jnp.concatenate(
        [
            (asg - target * per_owner + 1).astype(jnp.float32),
            (rank & 255).astype(jnp.float32),
            (rank >> 8).astype(jnp.float32),
            power_row,
            jnp.zeros((4, rows), jnp.float32),
        ],
        axis=0,
    ).astype(jnp.bfloat16)
    facts = dot_t(facts, place)
    packed = (dot(place, high) + dot(place, low)).astype(jnp.int32).astype(jnp.int16)
    for v in range(owners):
        mine = slice(v * capacity, (v + 1) * capacity)
        for c in range(tiles):
            packs[v][c * capacity : (c + 1) * capacity, :] = packed[
                mine, c * LANES : (c + 1) * LANES
            ]
        notes = jnp.concatenate(
            [facts[:, mine], jnp.zeros((8, LANES - capacity), jnp.float32)], axis=1
        )
        notes = jnp.concatenate([notes, jnp.zeros((META - 8, LANES), jnp.float32)], axis=0)
        packs[v][tiles * capacity :, :] = notes.astype(jnp.int32).astype(jnp.int16)
    slot_copy.wait()


def digest(chunks, capacity, width, high_ref, low_ref):
    tiles = width // LANES
    clus, codes, scales = [], [], []
    for pair in range(len(chunks) // 2):
        notes = [
            ref[tiles * capacity :, :].astype(jnp.int32).astype(jnp.float32)[:8, :capacity]
            for ref in chunks[2 * pair : 2 * pair + 2]
        ]
        notes = jnp.concatenate(notes, axis=1)
        clu = notes[0:1, :] - 1.0
        rank = notes[1:2, :] + 256.0 * notes[2:3, :]
        power = notes[3:4, :]
        scale = jnp.full_like(power, 1.0 / FULL)
        for step in STEPS:
            there = power >= step
            scale = jnp.where(there, scale * 2.0**-step, scale)
            power = jnp.where(there, power - step, power)
        clus.append(clu)
        codes.append(jnp.where(clu >= 0.0, clu * CODE + rank, -1.0))
        scales.append(scale)
    blocks = len(clus)
    cols = jnp.transpose(
        jnp.concatenate(
            codes + scales + [jnp.zeros((LANES - 2 * blocks, LANES), jnp.float32)], axis=0
        )
    )[:, : 2 * blocks]
    for i, ref in enumerate(chunks):
        here = slice(i * capacity, (i + 1) * capacity)
        for c in range(tiles):
            tile = ref[c * capacity : (c + 1) * capacity, :]
            high, low = halves(tile.astype(jnp.int32).astype(jnp.float32))
            high_ref[here, c * LANES : (c + 1) * LANES] = high
            low_ref[here, c * LANES : (c + 1) * LANES] = low
    rows = [jnp.concatenate(x, axis=1) for x in (clus, codes, scales)]
    return jnp.concatenate(rows + [jnp.zeros((5, rows[0].shape[1]), jnp.float32)], axis=0), cols


def part_sums(facts, per_owner, high_ref, low_ref):
    own = iota((per_owner, facts.shape[1]), 0).astype(jnp.float32) == facts[0:1, :]
    member = jnp.where(own, facts[2:3, :], 0.0).astype(jnp.bfloat16)
    return dot(member, high_ref[...]) + dot(member, low_ref[...])


def best_of(scores, cols, facts):
    base = facts[0:1, :] * CODE
    code = facts[1:2, :]
    blocks = cols.shape[1] // 2
    best = jnp.full((1, scores.shape[1]), NONE, jnp.float32)
    for i in range(blocks):
        key = cols[:, i : i + 1]
        found = scores[i * LANES : (i + 1) * LANES, :] * cols[:, blocks + i : blocks + i + 1]
        found = jnp.where((key >= base) & (key < code), found, NONE)
        best = jnp.maximum(best, jnp.max(found, axis=0, keepdims=True))
    return best


def early_kernel(owners, capacity, per_owner, width, *refs):
    chunks = refs[: owners // 2]
    high_ref, facts_ref, cols_ref, sums_ref, best_ref, low_ref = refs[owners // 2 :]
    facts, cols = digest(chunks, capacity, width, high_ref, low_ref)
    facts_ref[...] = facts
    cols_ref[...] = cols
    sums_ref[...] = part_sums(facts, per_owner, high_ref, low_ref)
    best_ref[...] = best_of(dot_t(high_ref[...], high_ref[...]), cols, facts)


def late_kernel(owners, capacity, per_owner, width, *refs):
    half = owners // 2
    chunks = refs[:half]
    old_ref, old_facts_ref, old_cols_ref, old_sums_ref, old_best_ref = refs[half : half + 5]
    high_ref, facts_ref, sums_ref, best_ref, low_ref = refs[half + 5 :]
    count = half * capacity
    new_ref = high_ref.at[count:, :]
    facts, cols = digest(chunks, capacity, width, new_ref, low_ref)
    high_ref[:count, :] = old_ref[...]
    old_facts = old_facts_ref[...]
    facts_ref[:, :count] = old_facts
    facts_ref[:, count:] = facts
    sums_ref[...] = old_sums_ref[...] + part_sums(facts, per_owner, new_ref, low_ref)
    scores = dot_t(high_ref[...], new_ref[...])
    best_ref[:, count:] = jnp.maximum(
        best_of(scores[:count, :], old_cols_ref[...], facts), best_of(scores[count:, :], cols, facts)
    )
    best_ref[:, :count] = jnp.maximum(
        old_best_ref[...], best_of(dot_t(new_ref[...], old_ref[...]), cols, old_facts)
    )


def last_kernel(owners, capacity, per_owner, width, *refs):
    chunks = refs[:owners]
    asked_ref, asked_facts_ref, old_sums_ref, old_best_ref = refs[owners : owners + 4]
    cent_ref, back_ref, high_ref, low_ref = refs[owners + 4 :]
    me = lax.axis_index(("rows", "feat"))
    facts, cols = digest(chunks, capacity, width, high_ref, low_ref)
    sums = old_sums_ref[...] + part_sums(facts, per_owner, high_ref, low_ref)
    cent = sums * lax.rsqrt(jnp.sum(sums * sums, axis=1, keepdims=True) + EPSILON)
    cent_ref[...] = cent
    asked = asked_ref[...]
    asked_facts = asked_facts_ref[...]
    scale = asked_facts[2:3, :]
    best = best_of(dot_t(high_ref[...], asked), cols, asked_facts)
    best = jnp.maximum(jnp.maximum(best, old_best_ref[...]) * scale, -1.0)
    fits = dot_t(jnp.concatenate(halves(cent), axis=0), asked)
    fits = fits[:per_owner, :] + fits[per_owner:, :]
    own = iota(fits.shape, 0).astype(jnp.float32) == asked_facts[0:1, :]
    near = jnp.sum(jnp.where(own, fits, 0.0), axis=0, keepdims=True) * scale
    for i, v in enumerate(FIRST):
        part = slice(i * capacity, (i + 1) * capacity)
        back_ref[pl.ds(me ^ v, 1), :] = jnp.concatenate([best[:, part], near[:, part]], axis=1)


def pick_kernel(owners, capacity, per_owner, back_ref, asg_ref, slot_ref, best_ref, near_ref):
    rows = asg_ref.shape[1]
    back = back_ref[...]
    for first in range(0, rows, LANES):
        here = slice(first, first + LANES)
        hits = iota((owners, LANES), 0) == lax.div(asg_ref[:, here], jnp.int32(per_owner))
        pos = jnp.broadcast_to(lax.rem(slot_ref[:, here], jnp.int32(capacity)), (owners, LANES))
        for start, ref in ((0, best_ref), (capacity, near_ref)):
            found = jnp.take_along_axis(back, pos + start, axis=1, mode="promise_in_bounds")
            ref[:, here] = jnp.sum(jnp.where(hits, found, 0.0), axis=0, keepdims=True)


def exchange_pairs(embeddings, assign, order):
    owners = lax.axis_size("rows") * lax.axis_size("feat")
    rows, width = embeddings.shape
    half = owners // 2
    capacity = 2 * rows // owners
    per_owner = K // owners
    slots = owners * capacity
    tall = width // LANES * capacity + META
    assign = assign.reshape(1, rows)
    order = order.reshape(1, rows)
    vmem = pl.BlockSpec(memory_space=pltpu.VMEM)
    hbm = pl.BlockSpec(memory_space=pltpu.HBM)
    params = pltpu.CompilerParams(vmem_limit_bytes=32 << 20)

    def full(*shape, dtype=jnp.float32):
        return jax.ShapeDtypeStruct(shape, dtype)

    *packs, slot = pl.pallas_call(
        functools.partial(pack_kernel, owners, capacity, per_owner),
        out_shape=[full(tall, LANES, dtype=jnp.int16)] * owners + [full(1, rows, dtype=jnp.int32)],
        in_specs=[vmem] * 3,
        out_specs=[vmem] * owners + [hbm],
        scratch_shapes=[pltpu.VMEM((1, rows), jnp.int32), pltpu.SemaphoreType.DMA],
        compiler_params=params,
        name="pack",
    )(embeddings, assign, order)
    got = [packs[0]] + [None] * (owners - 1)
    for v in range(1, owners):
        got[v] = lax.ppermute(packs[v], ("rows", "feat"), [(i, i ^ v) for i in range(owners)])
    other = [swapped(chunk, "sub", 0) for chunk in got]
    near = pl.pallas_call(
        functools.partial(early_kernel, owners, capacity, per_owner, width),
        out_shape=[
            full(slots // 2, width, dtype=jnp.bfloat16),
            full(8, slots // 2),
            full(LANES, slots // LANES),
            full(per_owner, width),
            full(1, slots // 2),
        ],
        in_specs=[vmem] * half,
        out_specs=[vmem] * 5,
        scratch_shapes=[pltpu.VMEM((slots // 2, width), jnp.bfloat16)],
        compiler_params=params,
        name="score_early",
    )(*[got[v] for v in FIRST[:half]])
    asked = pl.pallas_call(
        functools.partial(late_kernel, owners, capacity, per_owner, width),
        out_shape=[
            full(slots, width, dtype=jnp.bfloat16),
            full(8, slots),
            full(per_owner, width),
            full(1, slots),
        ],
        in_specs=[vmem] * (half + 5),
        out_specs=[vmem] * 4,
        scratch_shapes=[pltpu.VMEM((slots // 2, width), jnp.bfloat16)],
        compiler_params=params,
        name="score_late",
    )(*[got[v] for v in FIRST[half:]], *near)
    cent, back = pl.pallas_call(
        functools.partial(last_kernel, owners, capacity, per_owner, width),
        out_shape=[full(per_owner, width), full(owners, LANES)],
        in_specs=[vmem] * (owners + 4),
        out_specs=[vmem] * 2,
        scratch_shapes=[pltpu.VMEM((slots, width), jnp.bfloat16)] * 2,
        compiler_params=params,
        name="score_last",
    )(*[other[v] for v in FIRST], *asked)
    back = lax.all_to_all(back, ("rows", "feat"), split_axis=0, concat_axis=0, tiled=True)
    best, near = pl.pallas_call(
        functools.partial(pick_kernel, owners, capacity, per_owner),
        out_shape=[full(1, rows)] * 2,
        in_specs=[vmem] * 3,
        out_specs=[vmem] * 2,
        name="pick",
    )(back, assign, slot)
    return best.reshape(rows), near.reshape(rows), cent


def body(embeddings, assign, order):
    owners = lax.axis_size("rows") * lax.axis_size("feat")
    rows, width = embeddings.shape
    few = owners == 8 and 2 * rows // owners * 2 == LANES and width % LANES == 0
    return (exchange_pairs if few else exchange_all)(embeddings, assign, order)


def solution(mesh):
    return jax.shard_map(
        body,
        mesh=mesh,
        in_specs=(
            P(("groups", "rows", "feat", "sub"), None),
            P(("groups", "rows", "feat", "sub")),
            P(("groups", "rows", "feat", "sub")),
        ),
        out_specs=(
            P(("groups", "rows", "feat", "sub")),
            P(("groups", "rows", "feat", "sub")),
            P(("groups", "rows", "feat"), None),
        ),
        check_vma=False,
    )
```

```python
import functools

import jax
import jax.numpy as jnp
from jax import lax
from jax.experimental import pallas as pl
from jax.experimental.pallas import tpu as pltpu
from jax.sharding import PartitionSpec as P

K = 1024


EPSILON = 1e-06
LANES = 128
META = 16
FULL = 32768.0
STEPS = (32, 16, 8, 4, 2, 1)
CODE = 65536.0
NONE = -1e30
FIRST = (4, 1, 5, 2, 6, 3, 7, 0)


def swapped(shard, axis, distance):
    return lax.ppermute(shard, axis, [(i, i ^ 1 << distance) for i in range(lax.axis_size(axis))])


def unit_rows(values):
    return values * lax.rsqrt(jnp.sum(values * values, axis=1, keepdims=True) + EPSILON)


def best_against(q_vec, q_clu, q_ord, k_vec, k_clu, k_ord):
    scores = lax.dot_general(
        q_vec, k_vec, (((1,), (1,)), ((), ())), preferred_element_type=jnp.float32
    )
    allowed = (q_clu[:, None] == k_clu[None, :]) & (k_ord[None, :] < q_ord[:, None])
    return jnp.max(jnp.where(allowed, scores, -1.0), axis=1)


def cluster_sums(vectors, clusters, first_cluster, per_owner):
    local = clusters - first_cluster
    member = (jnp.arange(per_owner, dtype=jnp.int32)[:, None] == local[None, :]).astype(jnp.float32)
    return jnp.dot(
        member, vectors, precision=lax.Precision.HIGHEST, preferred_element_type=jnp.float32
    )


def exchange_all(embeddings, assign, order):
    owners = lax.axis_size("rows") * lax.axis_size("feat")
    rows_dev = embeddings.shape[0]
    width = embeddings.shape[1]
    capacity = 2 * rows_dev // owners
    per_owner = K // owners
    slots = owners * capacity
    here = lax.axis_index(("rows", "feat"))
    unit = unit_rows(embeddings)
    target = assign // per_owner
    hits = (target[:, None] == jnp.arange(owners, dtype=jnp.int32)[None, :]).astype(jnp.int32)
    before = jnp.cumsum(hits, axis=0) - hits
    slot = target * capacity + jnp.sum(before * hits, axis=1)
    send_clu = jnp.full((slots,), -1, jnp.int32).at[slot].set(assign)
    send_ord = jnp.zeros((slots,), jnp.int32).at[slot].set(order)
    send_wide = jnp.zeros((slots, width), jnp.float32).at[slot].set(unit)
    spread = functools.partial(
        lax.all_to_all, axis_name=("rows", "feat"), split_axis=0, concat_axis=0, tiled=True
    )
    wide_vec = spread(send_wide.reshape(owners, capacity, width)).reshape(slots, width)
    got_clu = spread(send_clu.reshape(owners, capacity)).reshape(slots)
    got_ord = spread(send_ord.reshape(owners, capacity)).reshape(slots)
    other_wide, other_clu, other_ord = swapped((wide_vec, got_clu, got_ord), "sub", 0)
    first_cluster = here * per_owner
    own_sums = cluster_sums(wide_vec, got_clu, first_cluster, per_owner)
    pair_sums = cluster_sums(other_wide, other_clu, first_cluster, per_owner)
    own_cent = unit_rows(own_sums + pair_sums)
    got_vec = wide_vec.astype(jnp.bfloat16)
    other_vec = other_wide.astype(jnp.bfloat16)
    block = min(512, slots)
    nblock = slots // block

    def per_block(pieces):
        q_vec, q_clu, q_ord = pieces
        first = best_against(q_vec, q_clu, q_ord, got_vec, got_clu, got_ord)
        second = best_against(q_vec, q_clu, q_ord, other_vec, other_clu, other_ord)
        return jnp.maximum(first, second)

    best = lax.map(
        per_block,
        (
            got_vec.reshape(nblock, block, width),
            got_clu.reshape(nblock, block),
            got_ord.reshape(nblock, block),
        ),
    ).reshape(slots)
    local = jnp.clip(got_clu - here * per_owner, 0, per_owner - 1)
    fits = jnp.dot(
        got_vec.astype(jnp.float32),
        own_cent.T,
        precision=lax.Precision.HIGHEST,
        preferred_element_type=jnp.float32,
    )
    pick = local[:, None] == jnp.arange(per_owner, dtype=jnp.int32)[None, :]
    near = jnp.sum(jnp.where(pick, fits, 0.0), axis=1)
    back_best = spread(best.reshape(owners, capacity))
    back_near = spread(near.reshape(owners, capacity))
    return (back_best.reshape(slots)[slot], back_near.reshape(slots)[slot], own_cent)


def iota(shape, dim):
    return lax.broadcasted_iota(jnp.int32, shape, dim)


def dot(a, b):
    return jnp.dot(a, b, preferred_element_type=jnp.float32)


def dot_t(a, b):
    return lax.dot_general(a, b, (((1,), (1,)), ((), ())), preferred_element_type=jnp.float32)


def halves(x):
    high = x.astype(jnp.bfloat16)
    return high, (x - high.astype(jnp.float32)).astype(jnp.bfloat16)


def earlier_kernel(earlier_ref):
    shape = earlier_ref.shape
    earlier_ref[...] = (iota(shape, 0) < iota(shape, 1)).astype(jnp.bfloat16)


def slots_of(owners, capacity, per_owner, asg, earlier):
    me = lax.axis_index(("rows", "feat"))
    target = lax.div(asg, jnp.int32(per_owner))
    hits = iota((owners, asg.shape[1]), 0) == target
    before = dot(hits.astype(jnp.bfloat16), earlier)
    pos = jnp.sum(jnp.where(hits, before, 0.0), axis=0, keepdims=True).astype(jnp.int32)
    return (target ^ me) * capacity + pos


def pack_kernel(owners, capacity, per_owner, emb_ref, asg_ref, ord_ref, earlier_ref, *packs):
    rows, width = emb_ref.shape
    slots = owners * capacity
    tiles = width // LANES
    asg = asg_ref[...]
    rank = ord_ref[...]
    slot = slots_of(owners, capacity, per_owner, asg, earlier_ref[...])
    place = (iota((slots, rows), 0) == slot).astype(jnp.bfloat16)
    x = emb_ref[...]
    unit = x * lax.rsqrt(jnp.sum(x * x, axis=1, keepdims=True) + EPSILON)
    top = jnp.max(jnp.abs(unit), axis=1, keepdims=True)
    scale = jnp.ones_like(top)
    power = jnp.zeros_like(top)
    for step in STEPS:
        small = top * (scale * 2.0**step) < 1.0
        scale = jnp.where(small, scale * 2.0**step, scale)
        power = jnp.where(small, power + step, power)
    coded = jnp.minimum(jnp.round(unit * (scale * FULL)), FULL - 1.0)
    high, low = halves(coded)
    power_row = jnp.transpose(jnp.broadcast_to(power, (rows, LANES)))[:1, :]
    facts = jnp.concatenate(
        [
            (lax.rem(asg, jnp.int32(per_owner)) + 1).astype(jnp.float32),
            (rank & 255).astype(jnp.float32),
            (rank >> 8).astype(jnp.float32),
            power_row,
            jnp.zeros((4, rows), jnp.float32),
        ],
        axis=0,
    ).astype(jnp.bfloat16)
    facts = dot_t(facts, place)
    packed = (dot(place, high) + dot(place, low)).astype(jnp.int32).astype(jnp.int16)
    for v in range(owners):
        mine = slice(v * capacity, (v + 1) * capacity)
        for c in range(tiles):
            packs[v][c * capacity : (c + 1) * capacity, :] = packed[
                mine, c * LANES : (c + 1) * LANES
            ]
        notes = jnp.concatenate(
            [facts[:, mine], jnp.zeros((8, LANES - capacity), jnp.float32)], axis=1
        )
        notes = jnp.concatenate([notes, jnp.zeros((META - 8, LANES), jnp.float32)], axis=0)
        packs[v][tiles * capacity :, :] = notes.astype(jnp.int32).astype(jnp.int16)


def digest(chunks, capacity, width, high_ref, low_ref):
    tiles = width // LANES
    clus, codes, scales = [], [], []
    for pair in range(len(chunks) // 2):
        notes = [
            ref[tiles * capacity :, :].astype(jnp.int32).astype(jnp.float32)[:8, :capacity]
            for ref in chunks[2 * pair : 2 * pair + 2]
        ]
        notes = jnp.concatenate(notes, axis=1)
        clu = notes[0:1, :] - 1.0
        rank = notes[1:2, :] + 256.0 * notes[2:3, :]
        power = notes[3:4, :]
        scale = jnp.full_like(power, 1.0 / FULL)
        for step in STEPS:
            there = power >= step
            scale = jnp.where(there, scale * 2.0**-step, scale)
            power = jnp.where(there, power - step, power)
        clus.append(clu)
        codes.append(jnp.where(clu >= 0.0, clu * CODE + rank, -1.0))
        scales.append(scale)
    blocks = len(clus)
    cols = jnp.transpose(
        jnp.concatenate(
            codes + scales + [jnp.zeros((LANES - 2 * blocks, LANES), jnp.float32)], axis=0
        )
    )[:, : 2 * blocks]
    for i, ref in enumerate(chunks):
        here = slice(i * capacity, (i + 1) * capacity)
        for c in range(tiles):
            tile = ref[c * capacity : (c + 1) * capacity, :]
            high, low = halves(tile.astype(jnp.int32).astype(jnp.float32))
            high_ref[here, c * LANES : (c + 1) * LANES] = high
            low_ref[here, c * LANES : (c + 1) * LANES] = low
    rows = [jnp.concatenate(x, axis=1) for x in (clus, codes, scales)]
    return jnp.concatenate(rows + [jnp.zeros((5, rows[0].shape[1]), jnp.float32)], axis=0), cols


def part_sums(facts, per_owner, high_ref, low_ref):
    own = iota((per_owner, facts.shape[1]), 0).astype(jnp.float32) == facts[0:1, :]
    member = jnp.where(own, facts[2:3, :], 0.0).astype(jnp.bfloat16)
    return dot(member, high_ref[...]) + dot(member, low_ref[...])


def best_of(scores, cols, facts):
    base = facts[0:1, :] * CODE
    code = facts[1:2, :]
    blocks = cols.shape[1] // 2
    best = jnp.full((1, scores.shape[1]), NONE, jnp.float32)
    for i in range(blocks):
        key = cols[:, i : i + 1]
        found = scores[i * LANES : (i + 1) * LANES, :] * cols[:, blocks + i : blocks + i + 1]
        found = jnp.where((key >= base) & (key < code), found, NONE)
        best = jnp.maximum(best, jnp.max(found, axis=0, keepdims=True))
    return best


def early_kernel(owners, capacity, per_owner, width, *refs):
    asg_ref, earlier_ref, *chunks = refs[: owners // 2 + 2]
    slot_ref, high_ref, facts_ref, cols_ref, sums_ref, best_ref, low_ref = refs[owners // 2 + 2 :]
    slot_ref[...] = slots_of(owners, capacity, per_owner, asg_ref[...], earlier_ref[...])
    facts, cols = digest(chunks, capacity, width, high_ref, low_ref)
    facts_ref[...] = facts
    cols_ref[...] = cols
    sums_ref[...] = part_sums(facts, per_owner, high_ref, low_ref)
    best_ref[...] = best_of(dot_t(high_ref[...], high_ref[...]), cols, facts)


def late_kernel(owners, capacity, per_owner, width, *refs):
    half = owners // 2
    chunks = refs[:half]
    old_ref, old_facts_ref, old_cols_ref, old_sums_ref, old_best_ref = refs[half : half + 5]
    high_ref, facts_ref, sums_ref, best_ref, low_ref = refs[half + 5 :]
    count = half * capacity
    new_ref = high_ref.at[count:, :]
    facts, cols = digest(chunks, capacity, width, new_ref, low_ref)
    high_ref[:count, :] = old_ref[...]
    old_facts = old_facts_ref[...]
    facts_ref[:, :count] = old_facts
    facts_ref[:, count:] = facts
    sums_ref[...] = old_sums_ref[...] + part_sums(facts, per_owner, new_ref, low_ref)
    scores = dot_t(high_ref[...], new_ref[...])
    best_ref[:, count:] = jnp.maximum(
        best_of(scores[:count, :], old_cols_ref[...], facts), best_of(scores[count:, :], cols, facts)
    )
    best_ref[:, :count] = jnp.maximum(
        old_best_ref[...], best_of(dot_t(new_ref[...], old_ref[...]), cols, old_facts)
    )


def last_kernel(owners, capacity, per_owner, width, *refs):
    chunks = refs[:owners]
    asked_ref, asked_facts_ref, old_sums_ref, old_best_ref = refs[owners : owners + 4]
    cent_ref, back_ref, high_ref, low_ref = refs[owners + 4 :]
    me = lax.axis_index(("rows", "feat"))
    facts, cols = digest(chunks, capacity, width, high_ref, low_ref)
    sums = old_sums_ref[...] + part_sums(facts, per_owner, high_ref, low_ref)
    cent = sums * lax.rsqrt(jnp.sum(sums * sums, axis=1, keepdims=True) + EPSILON)
    cent_ref[...] = cent
    asked = asked_ref[...]
    asked_facts = asked_facts_ref[...]
    scale = asked_facts[2:3, :]
    best = best_of(dot_t(high_ref[...], asked), cols, asked_facts)
    best = jnp.maximum(jnp.maximum(best, old_best_ref[...]) * scale, -1.0)
    fits = dot_t(jnp.concatenate(halves(cent), axis=0), asked)
    fits = fits[:per_owner, :] + fits[per_owner:, :]
    own = iota(fits.shape, 0).astype(jnp.float32) == asked_facts[0:1, :]
    near = jnp.sum(jnp.where(own, fits, 0.0), axis=0, keepdims=True) * scale
    for i, v in enumerate(FIRST):
        part = slice(i * capacity, (i + 1) * capacity)
        back_ref[pl.ds(me ^ v, 1), :] = jnp.concatenate([best[:, part], near[:, part]], axis=1)


def pick_kernel(owners, capacity, per_owner, back_ref, asg_ref, slot_ref, best_ref, near_ref):
    rows = asg_ref.shape[1]
    back = back_ref[...]
    for first in range(0, rows, LANES):
        here = slice(first, first + LANES)
        hits = iota((owners, LANES), 0) == lax.div(asg_ref[:, here], jnp.int32(per_owner))
        pos = jnp.broadcast_to(lax.rem(slot_ref[:, here], jnp.int32(capacity)), (owners, LANES))
        for start, ref in ((0, best_ref), (capacity, near_ref)):
            found = jnp.take_along_axis(back, pos + start, axis=1, mode="promise_in_bounds")
            ref[:, here] = jnp.sum(jnp.where(hits, found, 0.0), axis=0, keepdims=True)


def exchange_pairs(embeddings, assign, order):
    owners = lax.axis_size("rows") * lax.axis_size("feat")
    rows, width = embeddings.shape
    half = owners // 2
    capacity = 2 * rows // owners
    per_owner = K // owners
    slots = owners * capacity
    tall = width // LANES * capacity + META
    assign = assign.reshape(1, rows)
    order = order.reshape(1, rows)
    vmem = pl.BlockSpec(memory_space=pltpu.VMEM)
    params = pltpu.CompilerParams(vmem_limit_bytes=32 << 20)

    def full(*shape, dtype=jnp.float32):
        return jax.ShapeDtypeStruct(shape, dtype)

    earlier = pl.pallas_call(
        earlier_kernel,
        out_shape=full(rows, rows, dtype=jnp.bfloat16),
        out_specs=vmem,
        compiler_params=params,
        cost_estimate=pl.CostEstimate(flops=1 << 30, bytes_accessed=8 << 20, transcendentals=0),
        name="earlier",
    )()
    packs = pl.pallas_call(
        functools.partial(pack_kernel, owners, capacity, per_owner),
        out_shape=[full(tall, LANES, dtype=jnp.int16)] * owners,
        in_specs=[vmem] * 4,
        out_specs=[vmem] * owners,
        compiler_params=params,
        name="pack",
    )(embeddings, assign, order, earlier)
    got = [packs[0]] + [None] * (owners - 1)
    for v in range(1, owners):
        got[v] = lax.ppermute(packs[v], ("rows", "feat"), [(i, i ^ v) for i in range(owners)])
    slot, *near = pl.pallas_call(
        functools.partial(early_kernel, owners, capacity, per_owner, width),
        out_shape=[
            full(1, rows, dtype=jnp.int32),
            full(slots // 2, width, dtype=jnp.bfloat16),
            full(8, slots // 2),
            full(LANES, slots // LANES),
            full(per_owner, width),
            full(1, slots // 2),
        ],
        in_specs=[vmem] * (half + 2),
        out_specs=[vmem] * 6,
        scratch_shapes=[pltpu.VMEM((slots // 2, width), jnp.bfloat16)],
        compiler_params=params,
        name="score_early",
    )(assign, earlier, *[got[v] for v in FIRST[:half]])
    last = FIRST[-2]
    held, near = lax.optimization_barrier((got[last], near))
    other = [swapped(held if v == last else got[v], "sub", 0) for v in range(owners)]
    asked = pl.pallas_call(
        functools.partial(late_kernel, owners, capacity, per_owner, width),
        out_shape=[
            full(slots, width, dtype=jnp.bfloat16),
            full(8, slots),
            full(per_owner, width),
            full(1, slots),
        ],
        in_specs=[vmem] * (half + 5),
        out_specs=[vmem] * 4,
        scratch_shapes=[pltpu.VMEM((slots // 2, width), jnp.bfloat16)],
        compiler_params=params,
        name="score_late",
    )(*[got[v] for v in FIRST[half:]], *near)
    cent, back = pl.pallas_call(
        functools.partial(last_kernel, owners, capacity, per_owner, width),
        out_shape=[full(per_owner, width), full(owners, LANES)],
        in_specs=[vmem] * (owners + 4),
        out_specs=[vmem] * 2,
        scratch_shapes=[pltpu.VMEM((slots, width), jnp.bfloat16)] * 2,
        compiler_params=params,
        name="score_last",
    )(*[other[v] for v in FIRST], *asked)
    back = lax.all_to_all(back, ("rows", "feat"), split_axis=0, concat_axis=0, tiled=True)
    best, near = pl.pallas_call(
        functools.partial(pick_kernel, owners, capacity, per_owner),
        out_shape=[full(1, rows)] * 2,
        in_specs=[vmem] * 3,
        out_specs=[vmem] * 2,
        name="pick",
    )(back, assign, slot)
    return best.reshape(rows), near.reshape(rows), cent


def body(embeddings, assign, order):
    owners = lax.axis_size("rows") * lax.axis_size("feat")
    rows, width = embeddings.shape
    few = owners == 8 and 2 * rows // owners * 2 == LANES and width % LANES == 0
    return (exchange_pairs if few else exchange_all)(embeddings, assign, order)


def solution(mesh):
    return jax.shard_map(
        body,
        mesh=mesh,
        in_specs=(
            P(("groups", "rows", "feat", "sub"), None),
            P(("groups", "rows", "feat", "sub")),
            P(("groups", "rows", "feat", "sub")),
        ),
        out_specs=(
            P(("groups", "rows", "feat", "sub")),
            P(("groups", "rows", "feat", "sub")),
            P(("groups", "rows", "feat"), None),
        ),
        check_vma=False,
    )
```

```python
import functools

import jax
import jax.numpy as jnp
from jax import lax
from jax.experimental import pallas as pl
from jax.experimental.pallas import tpu as pltpu
from jax.sharding import PartitionSpec as P

K = 1024


EPSILON = 1e-06
LANES = 128
META = 16
FULL = 32768.0
GROUP = 128
STEPS = (32, 16, 8, 4, 2, 1)
CODE = 65536.0
NONE = -1e30
FIRST = (6, 1, 5, 2, 7, 3, 4, 0)
HELD = 6
EARLY = 4


def swapped(shard, axis, distance):
    return lax.ppermute(shard, axis, [(i, i ^ 1 << distance) for i in range(lax.axis_size(axis))])


def unit_rows(values):
    return values * lax.rsqrt(jnp.sum(values * values, axis=1, keepdims=True) + EPSILON)


def best_against(q_vec, q_clu, q_ord, k_vec, k_clu, k_ord):
    scores = lax.dot_general(
        q_vec, k_vec, (((1,), (1,)), ((), ())), preferred_element_type=jnp.float32
    )
    allowed = (q_clu[:, None] == k_clu[None, :]) & (k_ord[None, :] < q_ord[:, None])
    return jnp.max(jnp.where(allowed, scores, -1.0), axis=1)


def cluster_sums(vectors, clusters, first_cluster, per_owner):
    local = clusters - first_cluster
    member = (jnp.arange(per_owner, dtype=jnp.int32)[:, None] == local[None, :]).astype(jnp.float32)
    return jnp.dot(
        member, vectors, precision=lax.Precision.HIGHEST, preferred_element_type=jnp.float32
    )


def exchange_all(embeddings, assign, order):
    owners = lax.axis_size("rows") * lax.axis_size("feat")
    rows_dev = embeddings.shape[0]
    width = embeddings.shape[1]
    capacity = 2 * rows_dev // owners
    per_owner = K // owners
    slots = owners * capacity
    here = lax.axis_index(("rows", "feat"))
    unit = unit_rows(embeddings)
    target = assign // per_owner
    hits = (target[:, None] == jnp.arange(owners, dtype=jnp.int32)[None, :]).astype(jnp.int32)
    before = jnp.cumsum(hits, axis=0) - hits
    slot = target * capacity + jnp.sum(before * hits, axis=1)
    send_clu = jnp.full((slots,), -1, jnp.int32).at[slot].set(assign)
    send_ord = jnp.zeros((slots,), jnp.int32).at[slot].set(order)
    send_wide = jnp.zeros((slots, width), jnp.float32).at[slot].set(unit)
    spread = functools.partial(
        lax.all_to_all, axis_name=("rows", "feat"), split_axis=0, concat_axis=0, tiled=True
    )
    wide_vec = spread(send_wide.reshape(owners, capacity, width)).reshape(slots, width)
    got_clu = spread(send_clu.reshape(owners, capacity)).reshape(slots)
    got_ord = spread(send_ord.reshape(owners, capacity)).reshape(slots)
    other_wide, other_clu, other_ord = swapped((wide_vec, got_clu, got_ord), "sub", 0)
    first_cluster = here * per_owner
    own_sums = cluster_sums(wide_vec, got_clu, first_cluster, per_owner)
    pair_sums = cluster_sums(other_wide, other_clu, first_cluster, per_owner)
    own_cent = unit_rows(own_sums + pair_sums)
    got_vec = wide_vec.astype(jnp.bfloat16)
    other_vec = other_wide.astype(jnp.bfloat16)
    block = min(512, slots)
    nblock = slots // block

    def per_block(pieces):
        q_vec, q_clu, q_ord = pieces
        first = best_against(q_vec, q_clu, q_ord, got_vec, got_clu, got_ord)
        second = best_against(q_vec, q_clu, q_ord, other_vec, other_clu, other_ord)
        return jnp.maximum(first, second)

    best = lax.map(
        per_block,
        (
            got_vec.reshape(nblock, block, width),
            got_clu.reshape(nblock, block),
            got_ord.reshape(nblock, block),
        ),
    ).reshape(slots)
    local = jnp.clip(got_clu - here * per_owner, 0, per_owner - 1)
    fits = jnp.dot(
        got_vec.astype(jnp.float32),
        own_cent.T,
        precision=lax.Precision.HIGHEST,
        preferred_element_type=jnp.float32,
    )
    pick = local[:, None] == jnp.arange(per_owner, dtype=jnp.int32)[None, :]
    near = jnp.sum(jnp.where(pick, fits, 0.0), axis=1)
    back_best = spread(best.reshape(owners, capacity))
    back_near = spread(near.reshape(owners, capacity))
    return (back_best.reshape(slots)[slot], back_near.reshape(slots)[slot], own_cent)


def iota(shape, dim):
    return lax.broadcasted_iota(jnp.int32, shape, dim)


def dot(a, b):
    return jnp.dot(a, b, preferred_element_type=jnp.float32)


def dot_t(a, b):
    return lax.dot_general(a, b, (((1,), (1,)), ((), ())), preferred_element_type=jnp.float32)


def halves(x):
    high = x.astype(jnp.bfloat16)
    return high, (x - high.astype(jnp.float32)).astype(jnp.bfloat16)


def earlier_kernel(earlier_ref):
    shape = earlier_ref.shape
    earlier_ref[...] = (iota(shape, 0) < iota(shape, 1)).astype(jnp.bfloat16)


def slots_of(owners, capacity, per_owner, asg, earlier):
    me = lax.axis_index(("rows", "feat"))
    target = lax.div(asg, jnp.int32(per_owner))
    hits = iota((owners, asg.shape[1]), 0) == target
    before = dot(hits.astype(jnp.bfloat16), earlier)
    pos = jnp.sum(jnp.where(hits, before, 0.0), axis=0, keepdims=True).astype(jnp.int32)
    return (target ^ me) * capacity + pos


def pack_kernel(owners, capacity, per_owner, emb_ref, asg_ref, ord_ref, earlier_ref, *packs):
    rows, width = emb_ref.shape
    slots = owners * capacity
    tiles = width // LANES
    asg = asg_ref[...]
    rank = ord_ref[...]
    slot = slots_of(owners, capacity, per_owner, asg, earlier_ref[...])
    place = (iota((slots, rows), 0) == slot).astype(jnp.bfloat16)
    x = emb_ref[...]
    norm = lax.rsqrt(jnp.sum(x * x, axis=1, keepdims=True) + EPSILON)
    top = jnp.max(jnp.abs(x), axis=1, keepdims=True) * norm
    scale = jnp.ones_like(top)
    power = jnp.zeros_like(top)
    for step in STEPS:
        small = top * (scale * 2.0**step) < 1.0
        scale = jnp.where(small, scale * 2.0**step, scale)
        power = jnp.where(small, power + step, power)
    coded = jnp.minimum(jnp.round(x * (norm * (scale * FULL))), FULL - 1.0)
    high, low = halves(coded)
    power_row = jnp.transpose(jnp.broadcast_to(power, (rows, LANES)))[:1, :]
    facts = jnp.concatenate(
        [
            (lax.rem(asg, jnp.int32(per_owner)) + 1).astype(jnp.float32),
            (rank & 255).astype(jnp.float32),
            (rank >> 8).astype(jnp.float32),
            power_row,
            jnp.zeros((4, rows), jnp.float32),
        ],
        axis=0,
    ).astype(jnp.bfloat16)
    facts = dot_t(facts, place)
    packed = (dot(place, high) + dot(place, low)).astype(jnp.int32).astype(jnp.int16)
    for v in range(owners):
        mine = slice(v * capacity, (v + 1) * capacity)
        for c in range(tiles):
            packs[v][c * capacity : (c + 1) * capacity, :] = packed[
                mine, c * LANES : (c + 1) * LANES
            ]
        notes = jnp.concatenate(
            [facts[:, mine], jnp.zeros((8, LANES - capacity), jnp.float32)], axis=1
        )
        notes = jnp.concatenate([notes, jnp.zeros((META - 8, LANES), jnp.float32)], axis=0)
        packs[v][tiles * capacity :, :] = notes.astype(jnp.int32).astype(jnp.int16)


def digest(chunks, capacity, width, high_ref, low_ref):
    tiles = width // LANES
    clus, codes, scales = [], [], []
    for pair in range(len(chunks) // 2):
        notes = [
            ref[tiles * capacity :, :].astype(jnp.int32).astype(jnp.float32)[:8, :capacity]
            for ref in chunks[2 * pair : 2 * pair + 2]
        ]
        notes = jnp.concatenate(notes, axis=1)
        clu = notes[0:1, :] - 1.0
        rank = notes[1:2, :] + 256.0 * notes[2:3, :]
        power = notes[3:4, :]
        scale = jnp.full_like(power, 1.0 / FULL)
        for step in STEPS:
            there = power >= step
            scale = jnp.where(there, scale * 2.0**-step, scale)
            power = jnp.where(there, power - step, power)
        clus.append(clu)
        codes.append(jnp.where(clu >= 0.0, clu * CODE + rank, -1.0))
        scales.append(scale)
    blocks = len(clus)
    cols = jnp.transpose(
        jnp.concatenate(
            codes + scales + [jnp.zeros((LANES - 2 * blocks, LANES), jnp.float32)], axis=0
        )
    )[:, : 2 * blocks]
    for i, ref in enumerate(chunks):
        here = slice(i * capacity, (i + 1) * capacity)
        for c in range(tiles):
            tile = ref[c * capacity : (c + 1) * capacity, :]
            high, low = halves(tile.astype(jnp.int32).astype(jnp.float32))
            high_ref[here, c * LANES : (c + 1) * LANES] = high
            low_ref[here, c * LANES : (c + 1) * LANES] = low
    rows = [jnp.concatenate(x, axis=1) for x in (clus, codes, scales)]
    return jnp.concatenate(rows + [jnp.zeros((5, rows[0].shape[1]), jnp.float32)], axis=0), cols


def part_sums(facts, per_owner, high_ref, low_ref):
    count = facts.shape[1]
    step = min(count, GROUP)
    total = None
    for first in range(0, count, step):
        here = slice(first, first + step)
        own = iota((per_owner, step), 0).astype(jnp.float32) == facts[0:1, here]
        member = jnp.where(own, facts[2:3, here], 0.0).astype(jnp.bfloat16)
        part = dot(member, high_ref[here, :]) + dot(member, low_ref[here, :])
        total = part if total is None else total + part
    return total


def best_of(scores, cols, facts):
    base = facts[0:1, :] * CODE
    code = facts[1:2, :]
    blocks = cols.shape[1] // 2
    best = jnp.full((1, scores.shape[1]), NONE, jnp.float32)
    for i in range(blocks):
        key = cols[:, i : i + 1]
        found = scores[i * LANES : (i + 1) * LANES, :] * cols[:, blocks + i : blocks + i + 1]
        found = jnp.where((key >= base) & (key < code), found, NONE)
        best = jnp.maximum(best, jnp.max(found, axis=0, keepdims=True))
    return best


def early_kernel(owners, capacity, per_owner, width, *refs):
    asg_ref, earlier_ref, *chunks = refs[: EARLY + 2]
    slot_ref, high_ref, facts_ref, cols_ref, sums_ref, best_ref, low_ref = refs[EARLY + 2 :]
    slot_ref[...] = slots_of(owners, capacity, per_owner, asg_ref[...], earlier_ref[...])
    facts, cols = digest(chunks, capacity, width, high_ref, low_ref)
    facts_ref[...] = facts
    cols_ref[...] = cols
    sums_ref[...] = part_sums(facts, per_owner, high_ref, low_ref)
    best_ref[...] = best_of(dot_t(high_ref[...], high_ref[...]), cols, facts)


def late_kernel(owners, capacity, per_owner, width, *refs):
    count = owners - EARLY
    chunks = refs[:count]
    old_ref, old_facts_ref, old_cols_ref, old_sums_ref, old_best_ref = refs[count : count + 5]
    high_ref, facts_ref, sums_ref, best_ref, low_ref = refs[count + 5 :]
    old_rows = EARLY * capacity
    new_ref = high_ref.at[old_rows:, :]
    facts, cols = digest(chunks, capacity, width, new_ref, low_ref)
    high_ref[:old_rows, :] = old_ref[...]
    old_facts = old_facts_ref[...]
    facts_ref[:, :old_rows] = old_facts
    facts_ref[:, old_rows:] = facts
    sums_ref[...] = old_sums_ref[...] + part_sums(facts, per_owner, new_ref, low_ref)
    new = new_ref[...]
    best_ref[:, old_rows:] = jnp.maximum(
        best_of(dot_t(old_ref[...], new), old_cols_ref[...], facts),
        best_of(dot_t(new, new), cols, facts),
    )
    best_ref[:, :old_rows] = jnp.maximum(
        old_best_ref[...], best_of(dot_t(new, old_ref[...]), cols, old_facts)
    )


def last_kernel(owners, capacity, per_owner, width, *refs):
    chunks = refs[:owners]
    asked_ref, asked_facts_ref, old_sums_ref, old_best_ref = refs[owners : owners + 4]
    cent_ref, back_ref, high_ref, low_ref = refs[owners + 4 :]
    me = lax.axis_index(("rows", "feat"))
    facts, cols = digest(chunks, capacity, width, high_ref, low_ref)
    sums = old_sums_ref[...] + part_sums(facts, per_owner, high_ref, low_ref)
    cent = sums * lax.rsqrt(jnp.sum(sums * sums, axis=1, keepdims=True) + EPSILON)
    cent_ref[...] = cent
    asked = asked_ref[...]
    asked_facts = asked_facts_ref[...]
    scale = asked_facts[2:3, :]
    best = best_of(dot_t(high_ref[...], asked), cols, asked_facts)
    best = jnp.maximum(jnp.maximum(best, old_best_ref[...]) * scale, -1.0)
    fits = dot_t(jnp.concatenate(halves(cent), axis=0), asked)
    fits = fits[:per_owner, :] + fits[per_owner:, :]
    own = iota(fits.shape, 0).astype(jnp.float32) == asked_facts[0:1, :]
    near = jnp.sum(jnp.where(own, fits, 0.0), axis=0, keepdims=True) * scale
    for i, v in enumerate(FIRST):
        part = slice(i * capacity, (i + 1) * capacity)
        back_ref[pl.ds(me ^ v, 1), :] = jnp.concatenate([best[:, part], near[:, part]], axis=1)


def exchange_pairs(embeddings, assign, order):
    owners = lax.axis_size("rows") * lax.axis_size("feat")
    rows, width = embeddings.shape
    capacity = 2 * rows // owners
    per_owner = K // owners
    slots = owners * capacity
    tall = width // LANES * capacity + META
    assign = assign.reshape(1, rows)
    order = order.reshape(1, rows)
    vmem = pl.BlockSpec(memory_space=pltpu.VMEM)
    params = pltpu.CompilerParams(vmem_limit_bytes=32 << 20)

    def full(*shape, dtype=jnp.float32):
        return jax.ShapeDtypeStruct(shape, dtype)

    earlier = pl.pallas_call(
        earlier_kernel,
        out_shape=full(rows, rows, dtype=jnp.bfloat16),
        out_specs=vmem,
        compiler_params=params,
        cost_estimate=pl.CostEstimate(flops=1 << 30, bytes_accessed=8 << 20, transcendentals=0),
        name="earlier",
    )()
    packs = pl.pallas_call(
        functools.partial(pack_kernel, owners, capacity, per_owner),
        out_shape=[full(tall, LANES, dtype=jnp.int16)] * owners,
        in_specs=[vmem] * 4,
        out_specs=[vmem] * owners,
        compiler_params=params,
        name="pack",
    )(embeddings, assign, order, earlier)
    got = [packs[0]] + [None] * (owners - 1)
    for v in range(1, owners):
        got[v] = lax.ppermute(packs[v], ("rows", "feat"), [(i, i ^ v) for i in range(owners)])
    begun = EARLY * capacity
    slot, *near = pl.pallas_call(
        functools.partial(early_kernel, owners, capacity, per_owner, width),
        out_shape=[
            full(1, rows, dtype=jnp.int32),
            full(begun, width, dtype=jnp.bfloat16),
            full(8, begun),
            full(LANES, 2 * begun // LANES),
            full(per_owner, width),
            full(1, begun),
        ],
        in_specs=[vmem] * (EARLY + 2),
        out_specs=[vmem] * 6,
        scratch_shapes=[pltpu.VMEM((begun, width), jnp.bfloat16)],
        compiler_params=params,
        name="score_early",
    )(assign, earlier, *[got[v] for v in FIRST[:EARLY]])
    last = FIRST[HELD]
    held, near = lax.optimization_barrier((got[last], near))
    other = [swapped(held if v == last else got[v], "sub", 0) for v in range(owners)]
    asked = pl.pallas_call(
        functools.partial(late_kernel, owners, capacity, per_owner, width),
        out_shape=[
            full(slots, width, dtype=jnp.bfloat16),
            full(8, slots),
            full(per_owner, width),
            full(1, slots),
        ],
        in_specs=[vmem] * (owners - EARLY + 5),
        out_specs=[vmem] * 4,
        scratch_shapes=[pltpu.VMEM((slots - begun, width), jnp.bfloat16)],
        compiler_params=params,
        name="score_late",
    )(*[got[v] for v in FIRST[EARLY:]], *near)
    cent, back = pl.pallas_call(
        functools.partial(last_kernel, owners, capacity, per_owner, width),
        out_shape=[full(per_owner, width), full(owners, LANES)],
        in_specs=[vmem] * (owners + 4),
        out_specs=[vmem] * 2,
        scratch_shapes=[pltpu.VMEM((slots, width), jnp.bfloat16)] * 2,
        compiler_params=params,
        name="score_last",
    )(*[other[v] for v in FIRST], *asked)
    back = lax.all_to_all(back, ("rows", "feat"), split_axis=0, concat_axis=0, tiled=True)
    slot = slot.reshape(rows)
    pos = lax.rem(slot, jnp.int32(capacity))
    target = lax.div(assign.reshape(rows), jnp.int32(per_owner))
    hits = (target[None, :, None] == jnp.arange(owners, dtype=jnp.int32)[:, None, None]) & (
        pos[None, :, None] == jnp.arange(capacity, dtype=jnp.int32)[None, None, :]
    )
    best = jnp.sum(jnp.where(hits, back[:, None, :capacity], 0.0), axis=(0, 2))
    near = jnp.sum(jnp.where(hits, back[:, None, capacity:], 0.0), axis=(0, 2))
    return best.reshape(rows), near.reshape(rows), cent


def body(embeddings, assign, order):
    owners = lax.axis_size("rows") * lax.axis_size("feat")
    rows, width = embeddings.shape
    few = owners == 8 and 2 * rows // owners * 2 == LANES and width % LANES == 0
    return (exchange_pairs if few else exchange_all)(embeddings, assign, order)


def solution(mesh):
    return jax.shard_map(
        body,
        mesh=mesh,
        in_specs=(
            P(("groups", "rows", "feat", "sub"), None),
            P(("groups", "rows", "feat", "sub")),
            P(("groups", "rows", "feat", "sub")),
        ),
        out_specs=(
            P(("groups", "rows", "feat", "sub")),
            P(("groups", "rows", "feat", "sub")),
            P(("groups", "rows", "feat"), None),
        ),
        check_vma=False,
    )
```

```python
import functools

import jax
import jax.numpy as jnp
from jax import lax
from jax.experimental import pallas as pl
from jax.experimental.pallas import tpu as pltpu
from jax.sharding import PartitionSpec as P

K = 1024


EPSILON = 1e-06
LANES = 128
META = 16
FULL = 32768.0
STEPS = (32, 16, 8, 4, 2, 1)
CODE = 65536.0
NONE = -1e30
FIRST = (6, 1, 5, 2, 7, 3, 0, 4)
HELD = 7
EARLY = 4


def swapped(shard, axis, distance):
    return lax.ppermute(shard, axis, [(i, i ^ 1 << distance) for i in range(lax.axis_size(axis))])


def unit_rows(values):
    return values * lax.rsqrt(jnp.sum(values * values, axis=1, keepdims=True) + EPSILON)


def best_against(q_vec, q_clu, q_ord, k_vec, k_clu, k_ord):
    scores = lax.dot_general(
        q_vec, k_vec, (((1,), (1,)), ((), ())), preferred_element_type=jnp.float32
    )
    allowed = (q_clu[:, None] == k_clu[None, :]) & (k_ord[None, :] < q_ord[:, None])
    return jnp.max(jnp.where(allowed, scores, -1.0), axis=1)


def cluster_sums(vectors, clusters, first_cluster, per_owner):
    local = clusters - first_cluster
    member = (jnp.arange(per_owner, dtype=jnp.int32)[:, None] == local[None, :]).astype(jnp.float32)
    return jnp.dot(
        member, vectors, precision=lax.Precision.HIGHEST, preferred_element_type=jnp.float32
    )


def exchange_all(embeddings, assign, order):
    owners = lax.axis_size("rows") * lax.axis_size("feat")
    rows_dev = embeddings.shape[0]
    width = embeddings.shape[1]
    capacity = 2 * rows_dev // owners
    per_owner = K // owners
    slots = owners * capacity
    here = lax.axis_index(("rows", "feat"))
    unit = unit_rows(embeddings)
    target = assign // per_owner
    hits = (target[:, None] == jnp.arange(owners, dtype=jnp.int32)[None, :]).astype(jnp.int32)
    before = jnp.cumsum(hits, axis=0) - hits
    slot = target * capacity + jnp.sum(before * hits, axis=1)
    send_clu = jnp.full((slots,), -1, jnp.int32).at[slot].set(assign)
    send_ord = jnp.zeros((slots,), jnp.int32).at[slot].set(order)
    send_wide = jnp.zeros((slots, width), jnp.float32).at[slot].set(unit)
    spread = functools.partial(
        lax.all_to_all, axis_name=("rows", "feat"), split_axis=0, concat_axis=0, tiled=True
    )
    wide_vec = spread(send_wide.reshape(owners, capacity, width)).reshape(slots, width)
    got_clu = spread(send_clu.reshape(owners, capacity)).reshape(slots)
    got_ord = spread(send_ord.reshape(owners, capacity)).reshape(slots)
    other_wide, other_clu, other_ord = swapped((wide_vec, got_clu, got_ord), "sub", 0)
    first_cluster = here * per_owner
    own_sums = cluster_sums(wide_vec, got_clu, first_cluster, per_owner)
    pair_sums = cluster_sums(other_wide, other_clu, first_cluster, per_owner)
    own_cent = unit_rows(own_sums + pair_sums)
    got_vec = wide_vec.astype(jnp.bfloat16)
    other_vec = other_wide.astype(jnp.bfloat16)
    block = min(512, slots)
    nblock = slots // block

    def per_block(pieces):
        q_vec, q_clu, q_ord = pieces
        first = best_against(q_vec, q_clu, q_ord, got_vec, got_clu, got_ord)
        second = best_against(q_vec, q_clu, q_ord, other_vec, other_clu, other_ord)
        return jnp.maximum(first, second)

    best = lax.map(
        per_block,
        (
            got_vec.reshape(nblock, block, width),
            got_clu.reshape(nblock, block),
            got_ord.reshape(nblock, block),
        ),
    ).reshape(slots)
    local = jnp.clip(got_clu - here * per_owner, 0, per_owner - 1)
    fits = jnp.dot(
        got_vec.astype(jnp.float32),
        own_cent.T,
        precision=lax.Precision.HIGHEST,
        preferred_element_type=jnp.float32,
    )
    pick = local[:, None] == jnp.arange(per_owner, dtype=jnp.int32)[None, :]
    near = jnp.sum(jnp.where(pick, fits, 0.0), axis=1)
    back_best = spread(best.reshape(owners, capacity))
    back_near = spread(near.reshape(owners, capacity))
    return (back_best.reshape(slots)[slot], back_near.reshape(slots)[slot], own_cent)


def iota(shape, dim):
    return lax.broadcasted_iota(jnp.int32, shape, dim)


def dot(a, b):
    return jnp.dot(a, b, preferred_element_type=jnp.float32)


def dot_t(a, b):
    return lax.dot_general(a, b, (((1,), (1,)), ((), ())), preferred_element_type=jnp.float32)


def halves(x):
    high = x.astype(jnp.bfloat16)
    return high, (x - high.astype(jnp.float32)).astype(jnp.bfloat16)


def earlier_kernel(earlier_ref):
    shape = earlier_ref.shape
    earlier_ref[...] = (iota(shape, 0) < iota(shape, 1)).astype(jnp.bfloat16)


def slots_of(owners, capacity, per_owner, asg, earlier):
    me = lax.axis_index(("rows", "feat"))
    target = lax.div(asg, jnp.int32(per_owner))
    hits = iota((owners, asg.shape[1]), 0) == target
    before = dot(hits.astype(jnp.bfloat16), earlier)
    pos = jnp.sum(jnp.where(hits, before, 0.0), axis=0, keepdims=True).astype(jnp.int32)
    return (target ^ me) * capacity + pos


def pack_kernel(owners, capacity, per_owner, emb_ref, asg_ref, ord_ref, earlier_ref, *packs):
    rows, width = emb_ref.shape
    slots = owners * capacity
    tiles = width // LANES
    asg = asg_ref[...]
    rank = ord_ref[...]
    slot = slots_of(owners, capacity, per_owner, asg, earlier_ref[...])
    place = (iota((slots, rows), 0) == slot).astype(jnp.bfloat16)
    x = emb_ref[...]
    norm = lax.rsqrt(jnp.sum(x * x, axis=1, keepdims=True) + EPSILON)
    top = jnp.max(jnp.abs(x), axis=1, keepdims=True) * norm
    scale = jnp.ones_like(top)
    power = jnp.zeros_like(top)
    for step in STEPS:
        small = top * (scale * 2.0**step) < 1.0
        scale = jnp.where(small, scale * 2.0**step, scale)
        power = jnp.where(small, power + step, power)
    coded = jnp.minimum(jnp.round(x * (norm * (scale * FULL))), FULL - 1.0)
    high, low = halves(coded)
    power_row = jnp.transpose(jnp.broadcast_to(power, (rows, LANES)))[:1, :]
    facts = jnp.concatenate(
        [
            (lax.rem(asg, jnp.int32(per_owner)) + 1).astype(jnp.float32),
            (rank & 255).astype(jnp.float32),
            (rank >> 8).astype(jnp.float32),
            power_row,
            jnp.zeros((4, rows), jnp.float32),
        ],
        axis=0,
    ).astype(jnp.bfloat16)
    facts = dot_t(facts, place)
    packed = (dot(place, high) + dot(place, low)).astype(jnp.int32).astype(jnp.int16)
    for v in range(owners):
        mine = slice(v * capacity, (v + 1) * capacity)
        for c in range(tiles):
            packs[v][c * capacity : (c + 1) * capacity, :] = packed[
                mine, c * LANES : (c + 1) * LANES
            ]
        notes = jnp.concatenate(
            [facts[:, mine], jnp.zeros((8, LANES - capacity), jnp.float32)], axis=1
        )
        notes = jnp.concatenate([notes, jnp.zeros((META - 8, LANES), jnp.float32)], axis=0)
        packs[v][tiles * capacity :, :] = notes.astype(jnp.int32).astype(jnp.int16)


def digest(chunks, capacity, width, per_owner, high_ref):
    tiles = width // LANES
    clus, codes, scales = [], [], []
    sums = None
    for pair in range(len(chunks) // 2):
        notes = [
            ref[tiles * capacity :, :].astype(jnp.int32).astype(jnp.float32)[:8, :capacity]
            for ref in chunks[2 * pair : 2 * pair + 2]
        ]
        notes = jnp.concatenate(notes, axis=1)
        clu = notes[0:1, :] - 1.0
        rank = notes[1:2, :] + 256.0 * notes[2:3, :]
        power = notes[3:4, :]
        scale = jnp.full_like(power, 1.0 / FULL)
        for step in STEPS:
            there = power >= step
            scale = jnp.where(there, scale * 2.0**-step, scale)
            power = jnp.where(there, power - step, power)
        clus.append(clu)
        codes.append(jnp.where(clu >= 0.0, clu * CODE + rank, -1.0))
        scales.append(scale)
        own = iota((per_owner, LANES), 0).astype(jnp.float32) == clu
        member = jnp.where(own, scale, 0.0).astype(jnp.bfloat16)
        highs, lows = [], []
        for i in (2 * pair, 2 * pair + 1):
            ref = chunks[i]
            here = slice(i * capacity, (i + 1) * capacity)
            pieces = [
                halves(ref[c * capacity : (c + 1) * capacity, :].astype(jnp.int32).astype(jnp.float32))
                for c in range(tiles)
            ]
            high = jnp.concatenate([piece[0] for piece in pieces], axis=1)
            high_ref[here, :] = high
            highs.append(high)
            lows.append(jnp.concatenate([piece[1] for piece in pieces], axis=1))
        part = dot(member, jnp.concatenate(highs, axis=0)) + dot(
            member, jnp.concatenate(lows, axis=0)
        )
        sums = part if sums is None else sums + part
    blocks = len(clus)
    cols = jnp.transpose(
        jnp.concatenate(
            codes + scales + [jnp.zeros((LANES - 2 * blocks, LANES), jnp.float32)], axis=0
        )
    )[:, : 2 * blocks]
    rows = [jnp.concatenate(x, axis=1) for x in (clus, codes, scales)]
    rows = jnp.concatenate(rows + [jnp.zeros((5, rows[0].shape[1]), jnp.float32)], axis=0)
    return rows, cols, sums


def best_of(scores, cols, facts):
    base = facts[0:1, :] * CODE
    code = facts[1:2, :]
    blocks = cols.shape[1] // 2
    best = jnp.full((1, scores.shape[1]), NONE, jnp.float32)
    for i in range(blocks):
        key = cols[:, i : i + 1]
        found = scores[i * LANES : (i + 1) * LANES, :] * cols[:, blocks + i : blocks + i + 1]
        found = jnp.where((key >= base) & (key < code), found, NONE)
        best = jnp.maximum(best, jnp.max(found, axis=0, keepdims=True))
    return best


def early_kernel(owners, capacity, per_owner, width, *refs):
    asg_ref, earlier_ref, *chunks = refs[: EARLY + 2]
    slot_ref, high_ref, facts_ref, cols_ref, sums_ref, best_ref = refs[EARLY + 2 :]
    slot_ref[...] = slots_of(owners, capacity, per_owner, asg_ref[...], earlier_ref[...])
    facts, cols, sums = digest(chunks, capacity, width, per_owner, high_ref)
    facts_ref[...] = facts
    cols_ref[...] = cols
    sums_ref[...] = sums
    best_ref[...] = best_of(dot_t(high_ref[...], high_ref[...]), cols, facts)


def cross_kernel(owners, capacity, per_owner, width, *refs):
    chunks = refs[:EARLY]
    old_ref, old_facts_ref, old_cols_ref, old_sums_ref, old_best_ref = refs[EARLY : EARLY + 5]
    high_ref, facts_ref, cols_ref, sums_ref, best_ref = refs[EARLY + 5 :]
    count = EARLY * capacity
    new_ref = high_ref.at[count:, :]
    facts, cols, sums = digest(chunks, capacity, width, per_owner, new_ref)
    high_ref[:count, :] = old_ref[...]
    old_facts = old_facts_ref[...]
    facts_ref[:, :count] = old_facts
    facts_ref[:, count:] = facts
    old_cols = old_cols_ref[...]
    blocks = EARLY // 2
    cols_ref[...] = jnp.concatenate(
        [old_cols[:, :blocks], cols[:, :blocks], old_cols[:, blocks:], cols[:, blocks:]], axis=1
    )
    sums_ref[...] = old_sums_ref[...] + sums
    best = best_of(dot_t(new_ref[...], old_ref[...]), cols, old_facts)
    best_ref[...] = jnp.maximum(old_best_ref[...], best)


def late_kernel(owners, capacity, per_owner, width, *refs):
    chunks = refs[: owners - EARLY]
    old_ref, old_facts_ref, old_cols_ref, old_sums_ref, old_best_ref = refs[len(chunks) : len(chunks) + 5]
    high_ref, facts_ref, sums_ref, best_ref = refs[len(chunks) + 5 :]
    asked = EARLY * capacity
    new_ref = high_ref.at[asked:, :]
    facts, cols, sums = digest(chunks, capacity, width, per_owner, new_ref)
    high_ref[:asked, :] = old_ref[:asked, :]
    old_facts = old_facts_ref[:, :asked]
    facts_ref[:, :asked] = old_facts
    facts_ref[:, asked:] = facts
    sums_ref[...] = old_sums_ref[...] + sums
    new = new_ref[...]
    best_ref[:, asked:] = jnp.maximum(
        best_of(dot_t(old_ref[...], new), old_cols_ref[...], facts),
        best_of(dot_t(new, new), cols, facts),
    )
    best_ref[:, :asked] = jnp.maximum(
        old_best_ref[...], best_of(dot_t(new, old_ref[:asked, :]), cols, old_facts)
    )


def last_kernel(owners, capacity, per_owner, width, *refs):
    count = owners - EARLY
    chunks = refs[:count]
    asked_ref, asked_facts_ref, old_sums_ref, old_best_ref = refs[count : count + 4]
    cent_ref, back_ref, high_ref = refs[count + 4 :]
    me = lax.axis_index(("rows", "feat"))
    facts, cols, sums = digest(chunks, capacity, width, per_owner, high_ref)
    sums = old_sums_ref[...] + sums
    norm = lax.rsqrt(jnp.sum(sums * sums, axis=1, keepdims=True) + EPSILON)
    cent_ref[...] = sums * norm
    asked = asked_ref[...]
    asked_facts = asked_facts_ref[...]
    scale = asked_facts[2:3, :]
    best = best_of(dot_t(high_ref[...], asked), cols, asked_facts)
    best = jnp.maximum(jnp.maximum(best, old_best_ref[...]) * scale, -1.0)
    fits = dot_t(jnp.concatenate(halves(sums), axis=0), asked)
    fits = (fits[:per_owner, :] + fits[per_owner:, :]) * norm
    own = iota(fits.shape, 0).astype(jnp.float32) == asked_facts[0:1, :]
    near = jnp.sum(jnp.where(own, fits, 0.0), axis=0, keepdims=True) * scale
    for i, v in enumerate(FIRST):
        part = slice(i * capacity, (i + 1) * capacity)
        back_ref[pl.ds(me ^ v, 1), :] = jnp.concatenate([best[:, part], near[:, part]], axis=1)


def exchange_pairs(embeddings, assign, order):
    owners = lax.axis_size("rows") * lax.axis_size("feat")
    rows, width = embeddings.shape
    capacity = 2 * rows // owners
    per_owner = K // owners
    slots = owners * capacity
    tall = width // LANES * capacity + META
    assign = assign.reshape(1, rows)
    order = order.reshape(1, rows)
    vmem = pl.BlockSpec(memory_space=pltpu.VMEM)
    params = pltpu.CompilerParams(vmem_limit_bytes=32 << 20)

    def full(*shape, dtype=jnp.float32):
        return jax.ShapeDtypeStruct(shape, dtype)

    earlier = pl.pallas_call(
        earlier_kernel,
        out_shape=full(rows, rows, dtype=jnp.bfloat16),
        out_specs=vmem,
        compiler_params=params,
        cost_estimate=pl.CostEstimate(flops=1 << 30, bytes_accessed=8 << 20, transcendentals=0),
        name="earlier",
    )()
    packs = pl.pallas_call(
        functools.partial(pack_kernel, owners, capacity, per_owner),
        out_shape=[full(tall, LANES, dtype=jnp.int16)] * owners,
        in_specs=[vmem] * 4,
        out_specs=[vmem] * owners,
        compiler_params=params,
        name="pack",
    )(embeddings, assign, order, earlier)
    got = [packs[0]] + [None] * (owners - 1)
    for v in range(1, owners):
        got[v] = lax.ppermute(packs[v], ("rows", "feat"), [(i, i ^ v) for i in range(owners)])
    begun = EARLY * capacity
    slot, *old = pl.pallas_call(
        functools.partial(early_kernel, owners, capacity, per_owner, width),
        out_shape=[
            full(1, rows, dtype=jnp.int32),
            full(begun, width, dtype=jnp.bfloat16),
            full(8, begun),
            full(LANES, 2 * begun // LANES),
            full(per_owner, width),
            full(1, begun),
        ],
        in_specs=[vmem] * (EARLY + 2),
        out_specs=[vmem] * 6,
        compiler_params=params,
        name="score_early",
    )(assign, earlier, *[got[v] for v in FIRST[:EARLY]])
    other = {v: swapped(got[v], "sub", 0) for v in FIRST[:EARLY]}
    old = pl.pallas_call(
        functools.partial(cross_kernel, owners, capacity, per_owner, width),
        out_shape=[
            full(2 * begun, width, dtype=jnp.bfloat16),
            full(8, 2 * begun),
            full(LANES, 4 * begun // LANES),
            full(per_owner, width),
            full(1, begun),
        ],
        in_specs=[vmem] * (EARLY + 5),
        out_specs=[vmem] * 5,
        compiler_params=params,
        name="score_cross",
    )(*other.values(), *old)
    held, old = lax.optimization_barrier((got[FIRST[HELD]], old))
    rest = FIRST[EARLY:]
    other = [swapped(held if v == FIRST[HELD] else got[v], "sub", 0) for v in rest]
    asked = pl.pallas_call(
        functools.partial(late_kernel, owners, capacity, per_owner, width),
        out_shape=[
            full(slots, width, dtype=jnp.bfloat16),
            full(8, slots),
            full(per_owner, width),
            full(1, slots),
        ],
        in_specs=[vmem] * (len(rest) + 5),
        out_specs=[vmem] * 4,
        compiler_params=params,
        name="score_late",
    )(*[got[v] for v in rest], *old)
    cent, back = pl.pallas_call(
        functools.partial(last_kernel, owners, capacity, per_owner, width),
        out_shape=[full(per_owner, width), full(owners, LANES)],
        in_specs=[vmem] * (len(rest) + 4),
        out_specs=[vmem] * 2,
        scratch_shapes=[pltpu.VMEM((len(rest) * capacity, width), jnp.bfloat16)],
        compiler_params=params,
        name="score_last",
    )(*other, *asked)
    back = lax.all_to_all(back, ("rows", "feat"), split_axis=0, concat_axis=0, tiled=True)
    slot = slot.reshape(rows)
    pos = lax.rem(slot, jnp.int32(capacity))
    target = lax.div(assign.reshape(rows), jnp.int32(per_owner))
    hits = (target[None, :, None] == jnp.arange(owners, dtype=jnp.int32)[:, None, None]) & (
        pos[None, :, None] == jnp.arange(capacity, dtype=jnp.int32)[None, None, :]
    )
    best = jnp.sum(jnp.where(hits, back[:, None, :capacity], 0.0), axis=(0, 2))
    near = jnp.sum(jnp.where(hits, back[:, None, capacity:], 0.0), axis=(0, 2))
    return best.reshape(rows), near.reshape(rows), cent


def body(embeddings, assign, order):
    owners = lax.axis_size("rows") * lax.axis_size("feat")
    rows, width = embeddings.shape
    few = owners == 8 and 2 * rows // owners * 2 == LANES and width % LANES == 0
    return (exchange_pairs if few else exchange_all)(embeddings, assign, order)


def solution(mesh):
    return jax.shard_map(
        body,
        mesh=mesh,
        in_specs=(
            P(("groups", "rows", "feat", "sub"), None),
            P(("groups", "rows", "feat", "sub")),
            P(("groups", "rows", "feat", "sub")),
        ),
        out_specs=(
            P(("groups", "rows", "feat", "sub")),
            P(("groups", "rows", "feat", "sub")),
            P(("groups", "rows", "feat"), None),
        ),
        check_vma=False,
    )
```

```python
import functools

import jax
import jax.numpy as jnp
from jax import lax
from jax.experimental import pallas as pl
from jax.experimental.pallas import tpu as pltpu
from jax.sharding import PartitionSpec as P

K = 1024


EPSILON = 1e-06
LANES = 128
META = 16
FULL = 32768.0
STEPS = (32, 16, 8, 4, 2, 1)
CODE = 65536.0
NONE = -1e30
FIRST = (6, 1, 5, 2, 4, 3, 0, 7)
HELD = 4
EARLY = 4
TIED = (6, 1,)
CROSSED = (6, 1,)


def swapped(shard, axis, distance):
    return lax.ppermute(shard, axis, [(i, i ^ 1 << distance) for i in range(lax.axis_size(axis))])


def unit_rows(values):
    return values * lax.rsqrt(jnp.sum(values * values, axis=1, keepdims=True) + EPSILON)


def best_against(q_vec, q_clu, q_ord, k_vec, k_clu, k_ord):
    scores = lax.dot_general(
        q_vec, k_vec, (((1,), (1,)), ((), ())), preferred_element_type=jnp.float32
    )
    allowed = (q_clu[:, None] == k_clu[None, :]) & (k_ord[None, :] < q_ord[:, None])
    return jnp.max(jnp.where(allowed, scores, -1.0), axis=1)


def cluster_sums(vectors, clusters, first_cluster, per_owner):
    local = clusters - first_cluster
    member = (jnp.arange(per_owner, dtype=jnp.int32)[:, None] == local[None, :]).astype(jnp.float32)
    return jnp.dot(
        member, vectors, precision=lax.Precision.HIGHEST, preferred_element_type=jnp.float32
    )


def exchange_all(embeddings, assign, order):
    owners = lax.axis_size("rows") * lax.axis_size("feat")
    rows_dev = embeddings.shape[0]
    width = embeddings.shape[1]
    capacity = 2 * rows_dev // owners
    per_owner = K // owners
    slots = owners * capacity
    here = lax.axis_index(("rows", "feat"))
    unit = unit_rows(embeddings)
    target = assign // per_owner
    hits = (target[:, None] == jnp.arange(owners, dtype=jnp.int32)[None, :]).astype(jnp.int32)
    before = jnp.cumsum(hits, axis=0) - hits
    slot = target * capacity + jnp.sum(before * hits, axis=1)
    send_clu = jnp.full((slots,), -1, jnp.int32).at[slot].set(assign)
    send_ord = jnp.zeros((slots,), jnp.int32).at[slot].set(order)
    send_wide = jnp.zeros((slots, width), jnp.float32).at[slot].set(unit)
    spread = functools.partial(
        lax.all_to_all, axis_name=("rows", "feat"), split_axis=0, concat_axis=0, tiled=True
    )
    wide_vec = spread(send_wide.reshape(owners, capacity, width)).reshape(slots, width)
    got_clu = spread(send_clu.reshape(owners, capacity)).reshape(slots)
    got_ord = spread(send_ord.reshape(owners, capacity)).reshape(slots)
    other_wide, other_clu, other_ord = swapped((wide_vec, got_clu, got_ord), "sub", 0)
    first_cluster = here * per_owner
    own_sums = cluster_sums(wide_vec, got_clu, first_cluster, per_owner)
    pair_sums = cluster_sums(other_wide, other_clu, first_cluster, per_owner)
    own_cent = unit_rows(own_sums + pair_sums)
    got_vec = wide_vec.astype(jnp.bfloat16)
    other_vec = other_wide.astype(jnp.bfloat16)
    block = min(512, slots)
    nblock = slots // block

    def per_block(pieces):
        q_vec, q_clu, q_ord = pieces
        first = best_against(q_vec, q_clu, q_ord, got_vec, got_clu, got_ord)
        second = best_against(q_vec, q_clu, q_ord, other_vec, other_clu, other_ord)
        return jnp.maximum(first, second)

    best = lax.map(
        per_block,
        (
            got_vec.reshape(nblock, block, width),
            got_clu.reshape(nblock, block),
            got_ord.reshape(nblock, block),
        ),
    ).reshape(slots)
    local = jnp.clip(got_clu - here * per_owner, 0, per_owner - 1)
    fits = jnp.dot(
        got_vec.astype(jnp.float32),
        own_cent.T,
        precision=lax.Precision.HIGHEST,
        preferred_element_type=jnp.float32,
    )
    pick = local[:, None] == jnp.arange(per_owner, dtype=jnp.int32)[None, :]
    near = jnp.sum(jnp.where(pick, fits, 0.0), axis=1)
    back_best = spread(best.reshape(owners, capacity))
    back_near = spread(near.reshape(owners, capacity))
    return (back_best.reshape(slots)[slot], back_near.reshape(slots)[slot], own_cent)


def iota(shape, dim):
    return lax.broadcasted_iota(jnp.int32, shape, dim)


def dot(a, b):
    return jnp.dot(a, b, preferred_element_type=jnp.float32)


def dot_t(a, b):
    return lax.dot_general(a, b, (((1,), (1,)), ((), ())), preferred_element_type=jnp.float32)


def halves(x):
    high = x.astype(jnp.bfloat16)
    return high, (x - high.astype(jnp.float32)).astype(jnp.bfloat16)


def earlier_kernel(earlier_ref):
    shape = earlier_ref.shape
    earlier_ref[...] = (iota(shape, 0) < iota(shape, 1)).astype(jnp.bfloat16)


def slots_of(owners, capacity, per_owner, asg, earlier):
    me = lax.axis_index(("rows", "feat"))
    target = lax.div(asg, jnp.int32(per_owner))
    hits = iota((owners, asg.shape[1]), 0) == target
    before = dot(hits.astype(jnp.bfloat16), earlier)
    pos = jnp.sum(jnp.where(hits, before, 0.0), axis=0, keepdims=True).astype(jnp.int32)
    return (target ^ me) * capacity + pos


def pack_kernel(owners, capacity, per_owner, emb_ref, asg_ref, ord_ref, earlier_ref, *packs):
    rows, width = emb_ref.shape
    slots = owners * capacity
    tiles = width // LANES
    asg = asg_ref[...]
    rank = ord_ref[...]
    slot = slots_of(owners, capacity, per_owner, asg, earlier_ref[...])
    place = (iota((slots, rows), 0) == slot).astype(jnp.bfloat16)
    x = emb_ref[...]
    norm = lax.rsqrt(jnp.sum(x * x, axis=1, keepdims=True) + EPSILON)
    top = jnp.max(jnp.abs(x), axis=1, keepdims=True) * norm
    scale = jnp.ones_like(top)
    power = jnp.zeros_like(top)
    for step in STEPS:
        small = top * (scale * 2.0**step) < 1.0
        scale = jnp.where(small, scale * 2.0**step, scale)
        power = jnp.where(small, power + step, power)
    coded = jnp.minimum(jnp.round(x * (norm * (scale * FULL))), FULL - 1.0)
    high, low = halves(coded)
    power_row = jnp.transpose(jnp.broadcast_to(power, (rows, LANES)))[:1, :]
    facts = jnp.concatenate(
        [
            (lax.rem(asg, jnp.int32(per_owner)) + 1).astype(jnp.float32),
            (rank & 255).astype(jnp.float32),
            (rank >> 8).astype(jnp.float32),
            power_row,
            jnp.zeros((4, rows), jnp.float32),
        ],
        axis=0,
    ).astype(jnp.bfloat16)
    facts = dot_t(facts, place)
    packed = (dot(place, high) + dot(place, low)).astype(jnp.int32).astype(jnp.int16)
    for v in range(owners):
        mine = slice(v * capacity, (v + 1) * capacity)
        for c in range(tiles):
            packs[v][c * capacity : (c + 1) * capacity, :] = packed[
                mine, c * LANES : (c + 1) * LANES
            ]
        notes = jnp.concatenate(
            [facts[:, mine], jnp.zeros((8, LANES - capacity), jnp.float32)], axis=1
        )
        notes = jnp.concatenate([notes, jnp.zeros((META - 8, LANES), jnp.float32)], axis=0)
        packs[v][tiles * capacity :, :] = notes.astype(jnp.int32).astype(jnp.int16)


def digest(chunks, capacity, width, per_owner, high_ref):
    tiles = width // LANES
    clus, codes, scales = [], [], []
    sums = None
    for pair in range(len(chunks) // 2):
        notes = [
            ref[tiles * capacity :, :].astype(jnp.int32).astype(jnp.float32)[:8, :capacity]
            for ref in chunks[2 * pair : 2 * pair + 2]
        ]
        notes = jnp.concatenate(notes, axis=1)
        clu = notes[0:1, :] - 1.0
        rank = notes[1:2, :] + 256.0 * notes[2:3, :]
        power = notes[3:4, :]
        scale = jnp.full_like(power, 1.0 / FULL)
        for step in STEPS:
            there = power >= step
            scale = jnp.where(there, scale * 2.0**-step, scale)
            power = jnp.where(there, power - step, power)
        clus.append(clu)
        codes.append(jnp.where(clu >= 0.0, clu * CODE + rank, -1.0))
        scales.append(scale)
        own = iota((per_owner, LANES), 0).astype(jnp.float32) == clu
        member = jnp.where(own, scale, 0.0).astype(jnp.bfloat16)
        highs, lows = [], []
        for i in (2 * pair, 2 * pair + 1):
            ref = chunks[i]
            here = slice(i * capacity, (i + 1) * capacity)
            pieces = [
                halves(ref[c * capacity : (c + 1) * capacity, :].astype(jnp.int32).astype(jnp.float32))
                for c in range(tiles)
            ]
            high = jnp.concatenate([piece[0] for piece in pieces], axis=1)
            high_ref[here, :] = high
            highs.append(high)
            lows.append(jnp.concatenate([piece[1] for piece in pieces], axis=1))
        part = dot(member, jnp.concatenate(highs, axis=0)) + dot(
            member, jnp.concatenate(lows, axis=0)
        )
        sums = part if sums is None else sums + part
    blocks = len(clus)
    cols = jnp.transpose(
        jnp.concatenate(
            codes + scales + [jnp.zeros((LANES - 2 * blocks, LANES), jnp.float32)], axis=0
        )
    )[:, : 2 * blocks]
    rows = [jnp.concatenate(x, axis=1) for x in (clus, codes, scales)]
    rows = jnp.concatenate(rows + [jnp.zeros((5, rows[0].shape[1]), jnp.float32)], axis=0)
    return rows, cols, sums


def best_of(scores, cols, facts):
    base = facts[0:1, :] * CODE
    code = facts[1:2, :]
    blocks = cols.shape[1] // 2
    best = jnp.full((1, scores.shape[1]), NONE, jnp.float32)
    for i in range(blocks):
        key = cols[:, i : i + 1]
        found = scores[i * LANES : (i + 1) * LANES, :] * cols[:, blocks + i : blocks + i + 1]
        found = jnp.where((key >= base) & (key < code), found, NONE)
        best = jnp.maximum(best, jnp.max(found, axis=0, keepdims=True))
    return best


def early_kernel(owners, capacity, per_owner, width, *refs):
    asg_ref, earlier_ref, *chunks = refs[: EARLY + 2]
    slot_ref, high_ref, facts_ref, cols_ref, sums_ref, best_ref = refs[EARLY + 2 :]
    slot_ref[...] = slots_of(owners, capacity, per_owner, asg_ref[...], earlier_ref[...])
    facts, cols, sums = digest(chunks, capacity, width, per_owner, high_ref)
    facts_ref[...] = facts
    cols_ref[...] = cols
    sums_ref[...] = sums
    best_ref[...] = best_of(dot_t(high_ref[...], high_ref[...]), cols, facts)


def cross_kernel(owners, capacity, per_owner, width, *refs):
    cut = len(CROSSED)
    chunks = refs[:cut]
    old_ref, old_facts_ref, old_cols_ref, old_sums_ref, old_best_ref = refs[cut : cut + 5]
    high_ref, facts_ref, cols_ref, sums_ref, best_ref = refs[cut + 5 :]
    count = EARLY * capacity
    new_ref = high_ref.at[count:, :]
    facts, cols, sums = digest(chunks, capacity, width, per_owner, new_ref)
    high_ref[:count, :] = old_ref[...]
    old_facts = old_facts_ref[...]
    facts_ref[:, :count] = old_facts
    facts_ref[:, count:] = facts
    old_cols = old_cols_ref[...]
    blocks = EARLY // 2
    cols_ref[...] = jnp.concatenate(
        [old_cols[:, :blocks], cols[:, : cut // 2], old_cols[:, blocks:], cols[:, cut // 2 :]], axis=1
    )
    sums_ref[...] = old_sums_ref[...] + sums
    best = best_of(dot_t(new_ref[...], old_ref[...]), cols, old_facts)
    best_ref[...] = jnp.maximum(old_best_ref[...], best)


def late_kernel(owners, capacity, per_owner, width, *refs):
    chunks = refs[: owners - EARLY]
    old_ref, old_facts_ref, old_cols_ref, old_sums_ref, old_best_ref = refs[len(chunks) : len(chunks) + 5]
    high_ref, facts_ref, sums_ref, best_ref = refs[len(chunks) + 5 :]
    asked = EARLY * capacity
    new_ref = high_ref.at[asked:, :]
    facts, cols, sums = digest(chunks, capacity, width, per_owner, new_ref)
    high_ref[:asked, :] = old_ref[:asked, :]
    old_facts = old_facts_ref[:, :asked]
    facts_ref[:, :asked] = old_facts
    facts_ref[:, asked:] = facts
    sums_ref[...] = old_sums_ref[...] + sums
    new = new_ref[...]
    best_ref[:, asked:] = jnp.maximum(
        best_of(dot_t(old_ref[...], new), old_cols_ref[...], facts),
        best_of(dot_t(new, new), cols, facts),
    )
    best_ref[:, :asked] = jnp.maximum(
        old_best_ref[...], best_of(dot_t(new, old_ref[:asked, :]), cols, old_facts)
    )


def last_kernel(owners, capacity, per_owner, width, *refs):
    count = owners - len(CROSSED)
    chunks = refs[:count]
    asked_ref, asked_facts_ref, old_sums_ref, old_best_ref = refs[count : count + 4]
    cent_ref, back_ref, high_ref = refs[count + 4 :]
    me = lax.axis_index(("rows", "feat"))
    facts, cols, sums = digest(chunks, capacity, width, per_owner, high_ref)
    sums = old_sums_ref[...] + sums
    norm = lax.rsqrt(jnp.sum(sums * sums, axis=1, keepdims=True) + EPSILON)
    cent_ref[...] = sums * norm
    asked = asked_ref[...]
    asked_facts = asked_facts_ref[...]
    scale = asked_facts[2:3, :]
    best = best_of(dot_t(high_ref[...], asked), cols, asked_facts)
    best = jnp.maximum(jnp.maximum(best, old_best_ref[...]) * scale, -1.0)
    fits = dot_t(jnp.concatenate(halves(sums), axis=0), asked)
    fits = (fits[:per_owner, :] + fits[per_owner:, :]) * norm
    own = iota(fits.shape, 0).astype(jnp.float32) == asked_facts[0:1, :]
    near = jnp.sum(jnp.where(own, fits, 0.0), axis=0, keepdims=True) * scale
    for i, v in enumerate(FIRST):
        part = slice(i * capacity, (i + 1) * capacity)
        back_ref[pl.ds(me ^ v, 1), :] = jnp.concatenate([best[:, part], near[:, part]], axis=1)


def exchange_pairs(embeddings, assign, order):
    owners = lax.axis_size("rows") * lax.axis_size("feat")
    rows, width = embeddings.shape
    capacity = 2 * rows // owners
    per_owner = K // owners
    slots = owners * capacity
    tall = width // LANES * capacity + META
    assign = assign.reshape(1, rows)
    order = order.reshape(1, rows)
    vmem = pl.BlockSpec(memory_space=pltpu.VMEM)
    params = pltpu.CompilerParams(vmem_limit_bytes=32 << 20)

    def full(*shape, dtype=jnp.float32):
        return jax.ShapeDtypeStruct(shape, dtype)

    earlier = pl.pallas_call(
        earlier_kernel,
        out_shape=full(rows, rows, dtype=jnp.bfloat16),
        out_specs=vmem,
        compiler_params=params,
        cost_estimate=pl.CostEstimate(flops=1 << 30, bytes_accessed=8 << 20, transcendentals=0),
        name="earlier",
    )()
    packs = pl.pallas_call(
        functools.partial(pack_kernel, owners, capacity, per_owner),
        out_shape=[full(tall, LANES, dtype=jnp.int16)] * owners,
        in_specs=[vmem] * 4,
        out_specs=[vmem] * owners,
        compiler_params=params,
        name="pack",
    )(embeddings, assign, order, earlier)
    got = [packs[0]] + [None] * (owners - 1)
    for v in range(1, owners):
        got[v] = lax.ppermute(packs[v], ("rows", "feat"), [(i, i ^ v) for i in range(owners)])
    begun = EARLY * capacity
    slot, *old = pl.pallas_call(
        functools.partial(early_kernel, owners, capacity, per_owner, width),
        out_shape=[
            full(1, rows, dtype=jnp.int32),
            full(begun, width, dtype=jnp.bfloat16),
            full(8, begun),
            full(LANES, 2 * begun // LANES),
            full(per_owner, width),
            full(1, begun),
        ],
        in_specs=[vmem] * (EARLY + 2),
        out_specs=[vmem] * 6,
        compiler_params=params,
        name="score_early",
    )(assign, earlier, *[got[v] for v in FIRST[:EARLY]])
    tied, old = lax.optimization_barrier(([got[v] for v in TIED], old))
    tied = dict(zip(TIED, tied))
    other = [swapped(tied.get(v, got[v]), "sub", 0) for v in CROSSED]
    met = begun + len(CROSSED) * capacity
    old = pl.pallas_call(
        functools.partial(cross_kernel, owners, capacity, per_owner, width),
        out_shape=[
            full(met, width, dtype=jnp.bfloat16),
            full(8, met),
            full(LANES, 2 * met // LANES),
            full(per_owner, width),
            full(1, begun),
        ],
        in_specs=[vmem] * (len(CROSSED) + 5),
        out_specs=[vmem] * 5,
        compiler_params=params,
        name="score_cross",
    )(*other, *old)
    held, old = lax.optimization_barrier((got[FIRST[HELD]], old))
    tied[FIRST[HELD]] = held
    other = [swapped(tied.get(v, got[v]), "sub", 0) for v in FIRST if v not in CROSSED]
    rest = FIRST[EARLY:]
    asked = pl.pallas_call(
        functools.partial(late_kernel, owners, capacity, per_owner, width),
        out_shape=[
            full(slots, width, dtype=jnp.bfloat16),
            full(8, slots),
            full(per_owner, width),
            full(1, slots),
        ],
        in_specs=[vmem] * (len(rest) + 5),
        out_specs=[vmem] * 4,
        compiler_params=params,
        name="score_late",
    )(*[got[v] for v in rest], *old)
    cent, back = pl.pallas_call(
        functools.partial(last_kernel, owners, capacity, per_owner, width),
        out_shape=[full(per_owner, width), full(owners, LANES)],
        in_specs=[vmem] * (len(other) + 4),
        out_specs=[vmem] * 2,
        scratch_shapes=[pltpu.VMEM((len(other) * capacity, width), jnp.bfloat16)],
        compiler_params=params,
        name="score_last",
    )(*other, *asked)
    back = lax.all_to_all(back, ("rows", "feat"), split_axis=0, concat_axis=0, tiled=True)
    slot = slot.reshape(rows)
    pos = lax.rem(slot, jnp.int32(capacity))
    target = lax.div(assign.reshape(rows), jnp.int32(per_owner))
    hits = (target[None, :, None] == jnp.arange(owners, dtype=jnp.int32)[:, None, None]) & (
        pos[None, :, None] == jnp.arange(capacity, dtype=jnp.int32)[None, None, :]
    )
    best = jnp.sum(jnp.where(hits, back[:, None, :capacity], 0.0), axis=(0, 2))
    near = jnp.sum(jnp.where(hits, back[:, None, capacity:], 0.0), axis=(0, 2))
    return best.reshape(rows), near.reshape(rows), cent


def body(embeddings, assign, order):
    owners = lax.axis_size("rows") * lax.axis_size("feat")
    rows, width = embeddings.shape
    few = owners == 8 and 2 * rows // owners * 2 == LANES and width % LANES == 0
    return (exchange_pairs if few else exchange_all)(embeddings, assign, order)


def solution(mesh):
    return jax.shard_map(
        body,
        mesh=mesh,
        in_specs=(
            P(("groups", "rows", "feat", "sub"), None),
            P(("groups", "rows", "feat", "sub")),
            P(("groups", "rows", "feat", "sub")),
        ),
        out_specs=(
            P(("groups", "rows", "feat", "sub")),
            P(("groups", "rows", "feat", "sub")),
            P(("groups", "rows", "feat"), None),
        ),
        check_vma=False,
    )
```
